512 devices in a mesh: obj: 32 (over x, z), pat: 16 (over y, core).
Axes of the slice: x: 4, y: 8, z: 8, core: 2. Of those that a mesh axis runs over, the one named last changes fastest.
Arguments:
- obj_tiles: float32 [32, 2, 512, 512], P('obj', None, 'pat'), may hold values from -5 to 5
- probe_wave: float32 [2, 256, 256], replicated, may hold values from -6 to 6
- amplitudes: bfloat16 [32, 16, 4, 256, 256], P('obj', 'pat'), may hold values from 0.25 to 4
- offsets: int32 [32, 16, 4, 2], P('obj', 'pat'), may hold values from 0 to 504, as said below
- live_count: int32 [32, 16], P('obj', 'pat'), may hold values from 1 to 4, as said below
Outputs:
- object_step: float32 [32, 2, 512, 512], P('obj', None, 'pat')
The draws below stay inside these ranges and needn't reach their ends.
Inputs may be any that keep to these rules, and one draw needn't show every extreme that they name: `offsets`: multiples of 8; a patch starting there covers cells of its own tile and of the tiles to the right, below and below-right. Slots 0 to live_count - 1 of a device are used, the rest are not read.
All inputs are finite; a program needn't handle non-finite values.
Results may differ from the reference program's by a relative error of at most 0.012.
The reference program's roundings to bfloat16 on the way (of `half_way`, `corrected` and `half_back`) count: a program that leaves them out, or rounds other values in their place, can miss the bound.
Values sent between devices are 32-bit elements; how exact they have to be, the bound alone decides.
No kernel may reach another device: no remote copies, remote signals or barrier semaphores. Data moves between devices by JAX's collectives and lax.ppermute only.
A program may use at most 64 MiB of HBM per device.

```python
import math
import jax
import jax.numpy as jnp
from jax import lax

P_SIZE = 256
TILE = 512
GRID_C = 4
POS_DEV = 4
TILES = 32
WORKERS = 16


def draw_offsets(key, part):
    key = jax.random.fold_in(key, 11)
    first_key, second_key, third_key = jax.random.split(key, 3)
    corners = 8 * jax.random.randint(first_key, (TILES, WORKERS, POS_DEV, 2), 0, TILE // 8)
    tile_pick = jax.random.randint(second_key, (), 0, TILES)
    worker_pick = jax.random.randint(third_key, (), 0, WORKERS)
    extreme = jnp.array([TILE - 8, 0], dtype=jnp.int32)
    corners = corners.astype(jnp.int32).at[tile_pick, worker_pick, 0].set(extreme)
    return corners


def draw_live_count(key, part):
    key = jax.random.fold_in(key, 12)
    first_key, second_key, third_key, fourth_key = jax.random.split(key, 4)
    base_load = 1 + jax.random.randint(first_key, (TILES, WORKERS), 0, max(POS_DEV // 2, 1))
    full_load = jax.random.randint(second_key, (TILES, WORKERS), 0, 8) == 0
    counts = jnp.where(full_load, POS_DEV, base_load).astype(jnp.int32)
    tile_pick = jax.random.randint(third_key, (), 0, TILES)
    worker_pick = jax.random.randint(fourth_key, (), 0, WORKERS)
    return counts.at[tile_pick, worker_pick].set(POS_DEV)


def steps_of(own_key, dims, cuts, low, largest):
    def one(dim, blocks):
        steps = jax.random.uniform(jax.random.fold_in(jax.random.fold_in(own_key, 6), dim), (blocks,), jnp.float32, low / len(cuts), largest / len(cuts))
        return jnp.repeat(jnp.exp(steps), dims[dim] // blocks).reshape((-1,) + (1,) * (len(dims) - dim - 1))

    loudness = one(*cuts[0])
    for cut in cuts[1:]:
        loudness = loudness * one(*cut)
    return loudness


def centred(key, dims, width, limit, shards=(), held_as=jnp.bfloat16):
    factor_of = steps_of(key, dims, shards, -0.22, 0.18) if shards else 1.0
    entries = jax.random.normal(key, dims, jnp.float32) * width * factor_of
    return jnp.minimum(jnp.maximum(entries, -limit), limit).astype(held_as)


def setup_inputs(seed: int = 0) -> dict:
    key_of = jax.random.split(jax.random.key(seed), 6)
    obj_tiles = centred(key_of[0], (TILES, 2, TILE, TILE), 0.7, 5.0, ((0, 32), (2, 16)), jnp.float32)
    probe_wave = centred(key_of[1], (2, P_SIZE, P_SIZE), 1.0, 6.0, (), jnp.float32)
    amplitudes = jnp.clip(jnp.exp(math.log(4.0) - 2.7725887 * jax.random.uniform(key_of[2], (TILES, WORKERS, POS_DEV, P_SIZE, P_SIZE), jnp.float32) ** steps_of(key_of[2], (TILES, WORKERS, POS_DEV, P_SIZE, P_SIZE), ((0, 32), (1, 16)), -0.2, 0.2)), 0.25, 4.0).astype(jnp.bfloat16)
    offsets = draw_offsets(jax.random.fold_in(key_of[5], 71), 0)
    live_count = draw_live_count(jax.random.fold_in(key_of[5], 71), 0)
    return dict(obj_tiles=obj_tiles, probe_wave=probe_wave, amplitudes=amplitudes, offsets=offsets, live_count=live_count)


def dft_blocks(side_len):
    index_line = jnp.arange(side_len, dtype=jnp.int32)
    products = index_line[:, None] * index_line[None, :] % side_len
    angles = 2.0 * 3.141592653589793 / side_len * products.astype(jnp.float32)
    cos_part = jnp.cos(angles) / jnp.sqrt(jnp.float32(side_len))
    sin_part = -jnp.sin(angles) / jnp.sqrt(jnp.float32(side_len))
    left_table = jnp.concatenate([jnp.concatenate([cos_part, -sin_part], 1), jnp.concatenate([sin_part, cos_part], 1)], 0)
    right_table = jnp.concatenate([jnp.concatenate([cos_part, sin_part], 1), jnp.concatenate([-sin_part, cos_part], 1)], 0)
    return (left_table.astype(jnp.bfloat16), right_table.astype(jnp.bfloat16))

def position_terms(extended, row_at, col_at, probe_wave, pattern, left_table, right_table):
    side_len = probe_wave.shape[1]
    zero_at = jnp.zeros((), jnp.int32)
    patch_cells = lax.dynamic_slice(extended, (zero_at, row_at.astype(jnp.int32), col_at.astype(jnp.int32)), (2, side_len, side_len))
    probe_re = probe_wave[0]
    probe_im = probe_wave[1]
    wave_re = probe_re * patch_cells[0] - probe_im * patch_cells[1]
    wave_im = probe_re * patch_cells[1] + probe_im * patch_cells[0]
    wave_stack = jnp.concatenate([wave_re, wave_im], 0).astype(jnp.bfloat16)
    half_way = jnp.dot(left_table, wave_stack, preferred_element_type=jnp.float32).astype(jnp.bfloat16)
    half_side = jnp.concatenate([half_way[:side_len], half_way[side_len:]], 1)
    far_field = jnp.dot(half_side, right_table, preferred_element_type=jnp.float32)
    far_re = far_field[:, :side_len]
    far_im = far_field[:, side_len:]
    ratio_amp = pattern.astype(jnp.float32) / jnp.sqrt(far_re * far_re + far_im * far_im + 0.01)
    corrected = (far_field * jnp.concatenate([ratio_amp, ratio_amp], 1)).astype(jnp.bfloat16)
    half_back = jnp.dot(corrected, left_table, preferred_element_type=jnp.float32).astype(jnp.bfloat16)
    stacked_back = jnp.concatenate([half_back[:, :side_len], half_back[:, side_len:]], 0)
    near_field = jnp.dot(right_table, stacked_back, preferred_element_type=jnp.float32)
    delta_re = near_field[:side_len] - wave_re
    delta_im = near_field[side_len:] - wave_im
    return jnp.stack([probe_re * delta_re + probe_im * delta_im, probe_re * delta_im - probe_im * delta_re, probe_re * probe_re + probe_im * probe_im])

def reference(obj_tiles, probe_wave, amplitudes, offsets, live_count):
    rows_grid = TILES // GRID_C
    whole = obj_tiles.reshape(rows_grid, GRID_C, 2, TILE, TILE).transpose(2, 0, 3, 1, 4).reshape(2, rows_grid * TILE, GRID_C * TILE)
    whole = jnp.pad(whole, ((0, 0), (0, P_SIZE), (0, P_SIZE)))
    left_table, right_table = dft_blocks(P_SIZE)
    flat_index = jnp.arange(TILES * WORKERS * POS_DEV, dtype=jnp.int32)
    tile_ids = flat_index // (WORKERS * POS_DEV)
    slot_ids = flat_index % POS_DEV
    flat_amp = amplitudes.reshape(TILES * WORKERS * POS_DEV, P_SIZE, P_SIZE)
    flat_off = offsets.reshape(TILES * WORKERS * POS_DEV, 2)
    flat_live = jnp.repeat(live_count.reshape(TILES * WORKERS), POS_DEV)
    zero_at = jnp.zeros((), jnp.int32)

    def advance(totals, record):
        tile_id, slot, pattern, corner, live_now = record
        row_at = (tile_id // GRID_C * TILE + corner[0]).astype(jnp.int32)
        col_at = (tile_id % GRID_C * TILE + corner[1]).astype(jnp.int32)

        def add_terms(current_totals):
            terms = position_terms(whole, row_at, col_at, probe_wave, pattern, left_table, right_table)
            current = lax.dynamic_slice(current_totals, (zero_at, row_at, col_at), (3, P_SIZE, P_SIZE))
            return lax.dynamic_update_slice(current_totals, current + terms, (zero_at, row_at, col_at))

        def keep_totals(current_totals):
            return current_totals
        return (lax.cond(slot < live_now, add_terms, keep_totals, totals), None)
    start = jnp.zeros((3, rows_grid * TILE + P_SIZE, GRID_C * TILE + P_SIZE), jnp.float32)
    totals, _ = lax.scan(advance, start, (tile_ids, slot_ids, flat_amp, flat_off, flat_live))
    totals = totals[:, :rows_grid * TILE, :GRID_C * TILE]
    weights = totals[2] + 1.0
    step_field = jnp.stack([totals[0] / weights, totals[1] / weights])
    return step_field.reshape(2, rows_grid, TILE, GRID_C, TILE).transpose(1, 3, 0, 2, 4).reshape(TILES, 2, TILE, TILE)
```

```python
import jax
import jax.numpy as jnp
from jax import lax
from jax.experimental import pallas as pl
from jax.experimental.pallas import tpu as pltpu
from jax.sharding import PartitionSpec as P

GRID_C = 4
TILES = 32
WORKERS = 16
SLOTS = 4
SIDE = 256
TILE = 512
WIDE = TILE + SIDE
OWN = TILE // WORKERS
LOW = SIDE // WORKERS
ROWS = OWN + LOW
SPAN = SIDE + 128
PAD = 48


def dft_blocks(side_len):
    index_line = jnp.arange(side_len, dtype=jnp.int32)
    products = index_line[:, None] * index_line[None, :] % side_len
    angles = 2.0 * 3.141592653589793 / side_len * products.astype(jnp.float32)
    cos_part = jnp.cos(angles) / jnp.sqrt(jnp.float32(side_len))
    sin_part = -jnp.sin(angles) / jnp.sqrt(jnp.float32(side_len))
    left_table = jnp.concatenate(
        [jnp.concatenate([cos_part, -sin_part], 1), jnp.concatenate([sin_part, cos_part], 1)], 0
    )
    right_table = jnp.concatenate(
        [jnp.concatenate([cos_part, sin_part], 1), jnp.concatenate([-sin_part, cos_part], 1)], 0
    )
    return (left_table.astype(jnp.bfloat16), right_table.astype(jnp.bfloat16))


def low_row(worker):
    return TILE + worker % 8 * (2 * LOW) + worker // 8 * LOW


def slots_kernel(
    corners, live, parity, cells_hbm, probe, pattern, left, right,
    keep_hbm, send_hbm, cells, sums, wave, half, sem,
):
    fetches = []
    for worker in range(WORKERS):
        low = low_row(worker)
        fetches.append(pltpu.make_async_copy(
            cells_hbm.at[worker, 0:OWN], cells.at[OWN * worker:OWN * (worker + 1)], sem.at[2 * worker]))
        fetches.append(pltpu.make_async_copy(
            cells_hbm.at[worker, OWN:ROWS], cells.at[low:low + LOW], sem.at[2 * worker + 1]))
    for copy in fetches:
        copy.start()

    def clear(i, _):
        sums[pl.ds(pl.multiple_of(i * 16, 16), 16), :] = jnp.zeros((16, 2 * WIDE), jnp.float32)
        return 0

    lax.fori_loop(0, WIDE // 16, clear, 0)
    for copy in fetches:
        copy.wait()

    def one(slot, _):
        row = corners[slot, 0]
        col = corners[slot, 1]
        base = pl.multiple_of(col // 128 * 128, 128)
        shift = col % 128
        back = (SPAN - shift) % SPAN
        for i in range(4):
            here = slice(64 * i, 64 * i + 64)
            rows = pl.ds(pl.multiple_of(row + 64 * i, 8), 64)
            cell_re = pltpu.roll(cells[rows, pl.ds(base, SPAN)], back, 1)[:, :SIDE]
            cell_im = pltpu.roll(cells[rows, pl.ds(pl.multiple_of(base + WIDE, 128), SPAN)], back, 1)[:, :SIDE]
            probe_re = probe[0, here, :]
            probe_im = probe[1, here, :]
            wave[here, :] = (probe_re * cell_re - probe_im * cell_im).astype(jnp.bfloat16)
            wave[64 * i + SIDE:64 * i + SIDE + 64, :] = (
                probe_re * cell_im + probe_im * cell_re).astype(jnp.bfloat16)
        half_way = jnp.dot(left[...], wave[...], preferred_element_type=jnp.float32).astype(jnp.bfloat16)
        half[:, :SIDE] = half_way[:SIDE]
        half[:, SIDE:] = half_way[SIDE:]
        far = jnp.dot(half[...], right[...], preferred_element_type=jnp.float32)
        far_re = far[:, :SIDE]
        far_im = far[:, SIDE:]
        ratio = pattern[slot].astype(jnp.float32) * lax.rsqrt(far_re * far_re + far_im * far_im + 0.01)
        half[:, :SIDE] = (far_re * ratio).astype(jnp.bfloat16)
        half[:, SIDE:] = (far_im * ratio).astype(jnp.bfloat16)
        half_back = jnp.dot(half[...], left[...], preferred_element_type=jnp.float32).astype(jnp.bfloat16)
        wave[:SIDE, :] = half_back[:, :SIDE]
        wave[SIDE:, :] = half_back[:, SIDE:]
        near = jnp.dot(right[...], wave[...], preferred_element_type=jnp.float32)
        for i in range(4):
            here = slice(64 * i, 64 * i + 64)
            rows = pl.ds(pl.multiple_of(row + 64 * i, 8), 64)
            near_re = near[64 * i:64 * i + 64]
            near_im = near[64 * i + SIDE:64 * i + SIDE + 64]
            probe_re = probe[0, here, :]
            probe_im = probe[1, here, :]
            blank = jnp.zeros((64, 128), jnp.float32)
            term_re = jnp.concatenate([probe_re * near_re + probe_im * near_im, blank], 1)
            term_im = jnp.concatenate([probe_re * near_im - probe_im * near_re, blank], 1)
            sums[rows, pl.ds(base, SPAN)] += pltpu.roll(term_re, shift, 1)
            sums[rows, pl.ds(pl.multiple_of(base + WIDE, 128), SPAN)] += pltpu.roll(term_im, shift, 1)
        return 0

    lax.fori_loop(0, live[0, 0], one, 0)

    def store(own_core):
        copies = []
        for worker in range(WORKERS):
            low = low_row(worker)
            target = keep_hbm if worker % 2 == own_core else send_hbm
            copies.append(pltpu.make_async_copy(
                sums.at[OWN * worker:OWN * (worker + 1)], target.at[worker // 2, 0:OWN], sem.at[2 * worker]))
            copies.append(pltpu.make_async_copy(
                sums.at[low:low + LOW], target.at[worker // 2, OWN:ROWS], sem.at[2 * worker + 1]))
        for copy in copies:
            copy.start()
        for copy in copies:
            copy.wait()

    @pl.when(parity[0] == 0)
    def _():
        store(0)

    @pl.when(parity[0] != 0)
    def _():
        store(1)


def weight_kernel(corners, live, me, probe, weights, padded):
    padded[...] = jnp.zeros_like(padded)
    for i in range(4):
        here = slice(64 * i, 64 * i + 64)
        probe_re = probe[0, here, :]
        probe_im = probe[1, here, :]
        padded[PAD + 64 * i:PAD + 64 * i + 64, 0:SIDE] = probe_re * probe_re + probe_im * probe_im
    weights[...] = jnp.zeros_like(weights)
    worker = me[0]
    own_first = worker * OWN
    low_first = low_row(worker)

    def one(index, _):
        other = index // SLOTS
        slot = index % SLOTS
        row = corners[other, 2 * slot]
        used = slot < live[other]
        col = jnp.where(used, corners[other, 2 * slot + 1], 0)
        base = pl.multiple_of(col // 128 * 128, 128)
        shift = col % 128

        def part(first, count, at):
            start = jnp.where(used, jnp.clip(first - row + PAD, 0, PAD + SIDE), 0)
            piece = padded[pl.ds(pl.multiple_of(start, 8), count), :]
            weights[at:at + count, pl.ds(base, SPAN)] += pltpu.roll(piece, shift, 1)

        part(own_first, OWN, 0)
        part(low_first, LOW, OWN)
        return 0

    lax.fori_loop(0, WORKERS * SLOTS, one, 0)


def smem():
    return pl.BlockSpec(memory_space=pltpu.SMEM)


def vmem():
    return pl.BlockSpec(memory_space=pltpu.VMEM)


def hbm():
    return pl.BlockSpec(memory_space=pl.ANY)


def patch_sums(corners, live, parity, cells, probe, patterns, left, right):
    chunk = jax.ShapeDtypeStruct((WORKERS // 2, ROWS, 2 * WIDE), jnp.float32)
    return pl.pallas_call(
        slots_kernel,
        out_shape=(chunk, chunk),
        in_specs=[smem(), smem(), smem(), hbm(), vmem(), vmem(), vmem(), vmem()],
        out_specs=(hbm(), hbm()),
        scratch_shapes=[
            pltpu.VMEM((WIDE, 2 * WIDE), jnp.float32),
            pltpu.VMEM((WIDE, 2 * WIDE), jnp.float32),
            pltpu.VMEM((2 * SIDE, SIDE), jnp.bfloat16),
            pltpu.VMEM((SIDE, 2 * SIDE), jnp.bfloat16),
            pltpu.SemaphoreType.DMA((2 * WORKERS,)),
        ],
        compiler_params=pltpu.CompilerParams(vmem_limit_bytes=40 * 2**20),
        cost_estimate=pl.CostEstimate(flops=2 * 10**9, bytes_accessed=12 * 10**6, transcendentals=0),
        name="patch_sums",
    )(corners, live, parity, cells, probe, patterns, left, right)


def weight_rows(corners, live, me, probe):
    return pl.pallas_call(
        weight_kernel,
        out_shape=jax.ShapeDtypeStruct((ROWS, WIDE), jnp.float32),
        in_specs=[smem(), smem(), smem(), vmem()],
        out_specs=vmem(),
        scratch_shapes=[pltpu.VMEM((SIDE + 2 * PAD, SPAN), jnp.float32)],
        compiler_params=pltpu.CompilerParams(vmem_limit_bytes=16 * 2**20),
        cost_estimate=pl.CostEstimate(flops=10**7, bytes_accessed=10**6, transcendentals=0),
        name="weight_rows",
    )(corners, live, me, probe)


def moved(value, tile_step, pick):
    pairs = []
    for tile in range(TILES):
        for worker in range(WORKERS):
            target = pick(tile, worker)
            if target is not None and 0 <= tile + tile_step < TILES:
                pairs.append((tile * WORKERS + worker, (tile + tile_step) * WORKERS + target))
    return lax.ppermute(value, ("obj", "pat"), pairs)


def local(obj_tiles, probe_wave, amplitudes, offsets, live_count):
    own = obj_tiles[0]
    me = lax.axis_index("pat").astype(jnp.int32)
    corners = offsets[0, 0]

    own_left = jnp.concatenate([own[0, :, :SIDE], own[1, :, :SIDE]], 1)
    from_right = moved(own_left, -1, lambda tile, worker: worker if tile % GRID_C else None)
    spare_re = jnp.zeros((OWN, 8), jnp.float32)
    spare_re = spare_re.at[0].set(corners.reshape(8).astype(jnp.float32))
    spare_re = spare_re.at[1].set(jnp.broadcast_to(live_count[0, 0].astype(jnp.float32), (8,)))
    upper = jnp.concatenate(
        [own[0], from_right[:, :SIDE], own[1], from_right[:, SIDE:]], 1)
    low_a = moved(upper[:LOW], -GRID_C, lambda tile, worker: worker if worker < 8 else None)
    low_b = moved(upper[LOW:], -GRID_C, lambda tile, worker: worker + 8 if worker < 8 else None)
    marked = jnp.concatenate(
        [own[0], from_right[:, :SIDE - 8], spare_re, own[1], from_right[:, SIDE:]], 1)
    shard = jnp.concatenate([marked, low_a + low_b], 0)
    cells = lax.all_gather(shard, "pat", axis=0, tiled=True).reshape(WORKERS, ROWS, 2 * WIDE)

    left_table, right_table = dft_blocks(SIDE)
    keep, send = patch_sums(
        corners, live_count, (me % 2).reshape(1), cells, probe_wave, amplitudes[0, 0],
        left_table, right_table)
    other = lax.ppermute(send, "pat", [(i, i ^ 1) for i in range(WORKERS)])
    both = (keep + other).reshape(WORKERS // 2 * ROWS, 2 * WIDE)
    summed = lax.psum_scatter(
        both, "pat", scatter_dimension=0, tiled=True,
        axis_index_groups=[list(range(0, WORKERS, 2)), list(range(1, WORKERS, 2))])

    tile_corners = cells[:, 0, WIDE - 8:WIDE].astype(jnp.int32)
    tile_live = cells[:, 1, WIDE - 8].astype(jnp.int32)
    weights = weight_rows(tile_corners, tile_live, me.reshape(1), probe_wave)

    full = jnp.concatenate([summed, weights], 1)
    down_a = moved(full[OWN:], GRID_C, lambda tile, worker: worker if worker < 8 else None)
    down_b = moved(full[OWN:], GRID_C, lambda tile, worker: worker - 8 if worker >= 8 else None)
    upper_sum = (full[:OWN] + jnp.concatenate([down_a, down_b], 0)).reshape(OWN, 3, WIDE)
    to_right = upper_sum[:, :, TILE:].reshape(OWN, 3 * SIDE)
    from_left = moved(to_right, 1, lambda tile, worker: worker if tile % GRID_C != GRID_C - 1 else None)
    total = upper_sum[:, :, :TILE] + jnp.pad(
        from_left.reshape(OWN, 3, SIDE), ((0, 0), (0, 0), (0, TILE - SIDE)))
    weight = total[:, 2]
    over = 1.0 / (weight + 1.0)
    return jnp.stack([
        (total[:, 0] - weight * own[0]) * over,
        (total[:, 1] - weight * own[1]) * over,
    ])[None]


def solution(mesh):
    in_specs = (
        P("obj", None, "pat", None),
        P(),
        P("obj", "pat", None, None, None),
        P("obj", "pat", None, None),
        P("obj", "pat"),
    )
    out_specs = P("obj", None, "pat", None)
    return jax.shard_map(local, mesh=mesh, in_specs=in_specs, out_specs=out_specs, check_vma=False)
```

```python
import jax
import jax.numpy as jnp
from jax import lax
from jax.experimental import pallas as pl
from jax.experimental.pallas import tpu as pltpu
from jax.sharding import PartitionSpec as P

GRID_C = 4
TILES = 32
WORKERS = 16
SLOTS = 4
SIDE = 256
TILE = 512
WIDE = TILE + SIDE
OWN = TILE // WORKERS
LOW = SIDE // WORKERS
ROWS = OWN + LOW
SPAN = SIDE + 128
PAD = 48


def dft_blocks(side_len):
    index_line = jnp.arange(side_len, dtype=jnp.int32)
    products = index_line[:, None] * index_line[None, :] % side_len
    angles = 2.0 * 3.141592653589793 / side_len * products.astype(jnp.float32)
    cos_part = jnp.cos(angles) / jnp.sqrt(jnp.float32(side_len))
    sin_part = -jnp.sin(angles) / jnp.sqrt(jnp.float32(side_len))
    left_table = jnp.concatenate(
        [jnp.concatenate([cos_part, -sin_part], 1), jnp.concatenate([sin_part, cos_part], 1)], 0
    )
    right_table = jnp.concatenate(
        [jnp.concatenate([cos_part, sin_part], 1), jnp.concatenate([-sin_part, cos_part], 1)], 0
    )
    return (left_table.astype(jnp.bfloat16), right_table.astype(jnp.bfloat16))


def low_home(worker):
    upper_half = worker // 8
    y = worker // 2
    return 2 * (y + upper_half * (7 - 2 * y)) + worker % 2


def low_row(worker):
    return TILE + low_home(worker) * (2 * LOW) + worker // 8 * LOW


def slots_kernel(
    corners, live, parity, own_hbm, low_mine, low_other, probe, pattern, left, right,
    keep_own, send_own, keep_low, send_low, cells, sums, wave, half, sem,
):
    core = parity[0]
    fetches = [pltpu.make_async_copy(own_hbm, cells.at[0:TILE], sem.at[0])]
    low_rows = []
    for y in range(WORKERS // 2):
        mine = pl.multiple_of(low_row(2 * y + core), LOW)
        other = pl.multiple_of(low_row(2 * y + 1 - core), LOW)
        low_rows.append((mine, other))
        fetches.append(pltpu.make_async_copy(low_mine.at[y], cells.at[pl.ds(mine, LOW)], sem.at[1 + 2 * y]))
        fetches.append(pltpu.make_async_copy(low_other.at[y], cells.at[pl.ds(other, LOW)], sem.at[2 + 2 * y]))
    for copy in fetches:
        copy.start()

    def clear(i, _):
        sums[pl.ds(pl.multiple_of(i * 16, 16), 16), :] = jnp.zeros((16, 2 * WIDE), jnp.float32)
        return 0

    lax.fori_loop(0, WIDE // 16, clear, 0)
    for copy in fetches:
        copy.wait()

    def one(slot, _):
        row = corners[slot, 0]
        col = corners[slot, 1]
        base = pl.multiple_of(col // 128 * 128, 128)
        shift = col % 128
        back = (SPAN - shift) % SPAN
        for i in range(4):
            here = slice(64 * i, 64 * i + 64)
            rows = pl.ds(pl.multiple_of(row + 64 * i, 8), 64)
            cell_re = pltpu.roll(cells[rows, pl.ds(base, SPAN)], back, 1)[:, :SIDE]
            cell_im = pltpu.roll(cells[rows, pl.ds(pl.multiple_of(base + WIDE, 128), SPAN)], back, 1)[:, :SIDE]
            probe_re = probe[0, here, :]
            probe_im = probe[1, here, :]
            wave[here, :] = (probe_re * cell_re - probe_im * cell_im).astype(jnp.bfloat16)
            wave[64 * i + SIDE:64 * i + SIDE + 64, :] = (
                probe_re * cell_im + probe_im * cell_re).astype(jnp.bfloat16)
        half_way = jnp.dot(left[...], wave[...], preferred_element_type=jnp.float32).astype(jnp.bfloat16)
        half[:, :SIDE] = half_way[:SIDE]
        half[:, SIDE:] = half_way[SIDE:]
        far = jnp.dot(half[...], right[...], preferred_element_type=jnp.float32)
        far_re = far[:, :SIDE]
        far_im = far[:, SIDE:]
        ratio = pattern[slot].astype(jnp.float32) * lax.rsqrt(far_re * far_re + far_im * far_im + 0.01)
        half[:, :SIDE] = (far_re * ratio).astype(jnp.bfloat16)
        half[:, SIDE:] = (far_im * ratio).astype(jnp.bfloat16)
        half_back = jnp.dot(half[...], left[...], preferred_element_type=jnp.float32).astype(jnp.bfloat16)
        wave[:SIDE, :] = half_back[:, :SIDE]
        wave[SIDE:, :] = half_back[:, SIDE:]
        near = jnp.dot(right[...], wave[...], preferred_element_type=jnp.float32)
        for i in range(4):
            here = slice(64 * i, 64 * i + 64)
            rows = pl.ds(pl.multiple_of(row + 64 * i, 8), 64)
            near_re = near[64 * i:64 * i + 64]
            near_im = near[64 * i + SIDE:64 * i + SIDE + 64]
            probe_re = probe[0, here, :]
            probe_im = probe[1, here, :]
            blank = jnp.zeros((64, 128), jnp.float32)
            term_re = jnp.concatenate([probe_re * near_re + probe_im * near_im, blank], 1)
            term_im = jnp.concatenate([probe_re * near_im - probe_im * near_re, blank], 1)
            sums[rows, pl.ds(base, SPAN)] += pltpu.roll(term_re, shift, 1)
            sums[rows, pl.ds(pl.multiple_of(base + WIDE, 128), SPAN)] += pltpu.roll(term_im, shift, 1)
        return 0

    lax.fori_loop(0, live[0, 0], one, 0)

    copies = []
    for y in range(WORKERS // 2):
        mine, other = low_rows[y]
        own_mine = pl.multiple_of((2 * y + core) * OWN, OWN)
        own_other = pl.multiple_of((2 * y + 1 - core) * OWN, OWN)
        copies.append(pltpu.make_async_copy(sums.at[pl.ds(other, LOW)], send_low.at[y], sem.at[4 * y]))
        copies.append(pltpu.make_async_copy(sums.at[pl.ds(mine, LOW)], keep_low.at[y], sem.at[4 * y + 1]))
        copies.append(pltpu.make_async_copy(sums.at[pl.ds(own_other, OWN)], send_own.at[y], sem.at[4 * y + 2]))
        copies.append(pltpu.make_async_copy(sums.at[pl.ds(own_mine, OWN)], keep_own.at[y], sem.at[4 * y + 3]))
    for copy in copies:
        copy.start()
    for copy in copies:
        copy.wait()


def weight_kernel(corners, live, me, probe, weights, padded):
    padded[...] = jnp.zeros_like(padded)
    for i in range(4):
        here = slice(64 * i, 64 * i + 64)
        probe_re = probe[0, here, :]
        probe_im = probe[1, here, :]
        padded[PAD + 64 * i:PAD + 64 * i + 64, 0:SIDE] = probe_re * probe_re + probe_im * probe_im
    weights[...] = jnp.zeros_like(weights)
    worker = me[0]
    own_first = worker * OWN
    low_first = low_row(worker)

    def one(index, _):
        other = index // SLOTS
        slot = index % SLOTS
        row = corners[other, 2 * slot]
        used = slot < live[other]
        col = jnp.where(used, corners[other, 2 * slot + 1], 0)
        base = pl.multiple_of(col // 128 * 128, 128)
        shift = col % 128

        def part(first, count, at):
            start = jnp.where(used, jnp.clip(first - row + PAD, 0, PAD + SIDE), 0)
            piece = padded[pl.ds(pl.multiple_of(start, 8), count), :]
            weights[at:at + count, pl.ds(base, SPAN)] += pltpu.roll(piece, shift, 1)

        part(own_first, OWN, 0)
        part(low_first, LOW, OWN)
        return 0

    lax.fori_loop(0, WORKERS * SLOTS, one, 0)


def smem():
    return pl.BlockSpec(memory_space=pltpu.SMEM)


def vmem():
    return pl.BlockSpec(memory_space=pltpu.VMEM)


def hbm():
    return pl.BlockSpec(memory_space=pl.ANY)


def patch_sums(corners, live, parity, own_cells, low_mine, low_other, probe, patterns, left, right):
    own_chunk = jax.ShapeDtypeStruct((WORKERS // 2, OWN, 2 * WIDE), jnp.float32)
    low_chunk = jax.ShapeDtypeStruct((WORKERS // 2, LOW, 2 * WIDE), jnp.float32)
    return pl.pallas_call(
        slots_kernel,
        out_shape=(own_chunk, own_chunk, low_chunk, low_chunk),
        in_specs=[smem(), smem(), smem(), pl.BlockSpec(memory_space=pltpu.HBM), hbm(), hbm(),
                  vmem(), vmem(), vmem(), vmem()],
        out_specs=(hbm(), hbm(), hbm(), hbm()),
        scratch_shapes=[
            pltpu.VMEM((WIDE, 2 * WIDE), jnp.float32),
            pltpu.VMEM((WIDE, 2 * WIDE), jnp.float32),
            pltpu.VMEM((2 * SIDE, SIDE), jnp.bfloat16),
            pltpu.VMEM((SIDE, 2 * SIDE), jnp.bfloat16),
            pltpu.SemaphoreType.DMA((2 * WORKERS,)),
        ],
        compiler_params=pltpu.CompilerParams(vmem_limit_bytes=40 * 2**20),
        cost_estimate=pl.CostEstimate(flops=2 * 10**9, bytes_accessed=12 * 10**6, transcendentals=0),
        name="patch_sums",
    )(corners, live, parity, own_cells, low_mine, low_other, probe, patterns, left, right)


def weight_rows(corners, live, me, probe):
    return pl.pallas_call(
        weight_kernel,
        out_shape=jax.ShapeDtypeStruct((ROWS, WIDE), jnp.float32),
        in_specs=[smem(), smem(), smem(), vmem()],
        out_specs=vmem(),
        scratch_shapes=[pltpu.VMEM((SIDE + 2 * PAD, SPAN), jnp.float32)],
        compiler_params=pltpu.CompilerParams(vmem_limit_bytes=16 * 2**20),
        cost_estimate=pl.CostEstimate(flops=10**7, bytes_accessed=10**6, transcendentals=0),
        name="weight_rows",
    )(corners, live, me, probe)


def moved(value, tile_step, pick):
    pairs = []
    for tile in range(TILES):
        for worker in range(WORKERS):
            target = pick(tile, worker)
            if target is not None and 0 <= tile + tile_step < TILES:
                pairs.append((tile * WORKERS + worker, (tile + tile_step) * WORKERS + target))
    return lax.ppermute(value, ("obj", "pat"), pairs)


def local(obj_tiles, probe_wave, amplitudes, offsets, live_count):
    own = obj_tiles[0]
    me = lax.axis_index("pat").astype(jnp.int32)
    corners = offsets[0, 0]

    own_left = jnp.concatenate([own[0, :, :SIDE], own[1, :, :SIDE]], 1)
    from_right = moved(own_left, -1, lambda tile, worker: worker if tile % GRID_C else None)
    spare_re = jnp.zeros((OWN, 8), jnp.float32)
    spare_re = spare_re.at[0].set(corners.reshape(8).astype(jnp.float32))
    spare_re = spare_re.at[1].set(jnp.broadcast_to(live_count[0, 0].astype(jnp.float32), (8,)))
    shard = jnp.concatenate(
        [own[0], from_right[:, :SIDE - 8], spare_re, own[1], from_right[:, SIDE:]], 1)
    own_cells = lax.all_gather(shard, "pat", axis=0, tiled=True)
    mirrored = lambda worker: 2 * (7 - worker // 2) + worker % 2
    low_a = moved(shard[:LOW], -GRID_C, lambda tile, worker: worker if worker < 8 else None)
    low_b = moved(shard[LOW:], -GRID_C, lambda tile, worker: mirrored(worker) if worker < 8 else None)
    same_core = [list(range(0, WORKERS, 2)), list(range(1, WORKERS, 2))]
    sibling = [(i, i ^ 1) for i in range(WORKERS)]
    low_mine = lax.all_to_all(
        jnp.broadcast_to(low_a + low_b, (WORKERS // 2, LOW, 2 * WIDE)), "pat", 0, 0, axis_index_groups=same_core)
    low_other = lax.ppermute(low_mine, "pat", sibling)

    left_table, right_table = dft_blocks(SIDE)
    keep_own, send_own, keep_low, send_low = patch_sums(
        corners, live_count, (me % 2).reshape(1), own_cells, low_mine, low_other, probe_wave, amplitudes[0, 0],
        left_table, right_table)
    other_low = lax.ppermute(send_low, "pat", sibling)
    other_own = lax.ppermute(send_own, "pat", sibling)
    both_own = (keep_own + other_own).reshape(WORKERS // 2 * OWN, 2 * WIDE)
    both_low = keep_low + other_low
    both_own, both_low = lax.optimization_barrier((both_own, both_low))
    summed_own = lax.psum_scatter(
        both_own, "pat", scatter_dimension=0, tiled=True, axis_index_groups=same_core)

    by_tile = own_cells.reshape(WORKERS, OWN, 2 * WIDE)
    tile_corners = by_tile[:, 0, WIDE - 8:WIDE].astype(jnp.int32)
    tile_live = by_tile[:, 1, WIDE - 8].astype(jnp.int32)
    weights = weight_rows(tile_corners, tile_live, me.reshape(1), probe_wave)

    summed_low = jnp.sum(lax.all_to_all(both_low, "pat", 0, 0, axis_index_groups=same_core), 0)
    low = jnp.concatenate([summed_low, weights[OWN:]], 1)
    down_a = moved(low, GRID_C, lambda tile, worker: worker if worker < 8 else None)
    down_b = moved(low, GRID_C, lambda tile, worker: mirrored(worker) if worker >= 8 else None)
    upper_sum = (
        jnp.concatenate([summed_own, weights[:OWN]], 1) + jnp.concatenate([down_a, down_b], 0)
    ).reshape(OWN, 3, WIDE)
    to_right = upper_sum[:, :, TILE:].reshape(OWN, 3 * SIDE)
    from_left = moved(to_right, 1, lambda tile, worker: worker if tile % GRID_C != GRID_C - 1 else None)
    total = upper_sum[:, :, :TILE] + jnp.pad(
        from_left.reshape(OWN, 3, SIDE), ((0, 0), (0, 0), (0, TILE - SIDE)))
    weight = total[:, 2]
    over = 1.0 / (weight + 1.0)
    return jnp.stack([
        (total[:, 0] - weight * own[0]) * over,
        (total[:, 1] - weight * own[1]) * over,
    ])[None]


def solution(mesh):
    in_specs = (
        P("obj", None, "pat", None),
        P(),
        P("obj", "pat", None, None, None),
        P("obj", "pat", None, None),
        P("obj", "pat"),
    )
    out_specs = P("obj", None, "pat", None)
    return jax.shard_map(local, mesh=mesh, in_specs=in_specs, out_specs=out_specs, check_vma=False)
```

```python
import jax
import jax.numpy as jnp
import numpy as np
from jax import lax
from jax.experimental import pallas as pl
from jax.experimental.pallas import tpu as pltpu
from jax.sharding import PartitionSpec as P

GRID_C = 4
TILES = 32
WORKERS = 16
SLOTS = 4
SIDE = 256
TILE = 512
WIDE = TILE + SIDE
OWN = TILE // WORKERS
LOW = SIDE // WORKERS
ROWS = OWN + LOW
SPAN = SIDE + 128
PAD = 48


def dft_blocks(side_len):
    index_line = np.arange(side_len)
    products = index_line[:, None] * index_line[None, :] % side_len
    angles = (2.0 * np.pi / side_len) * products
    cos_part = np.cos(angles) / np.sqrt(side_len)
    sin_part = -np.sin(angles) / np.sqrt(side_len)
    left_table = np.block([[cos_part, -sin_part], [sin_part, cos_part]])
    right_table = np.block([[cos_part, sin_part], [-sin_part, cos_part]])
    return tuple(jnp.asarray(table.astype(np.float32).astype(jnp.bfloat16)) for table in (left_table, right_table))


def low_home(worker):
    upper_half = worker // 8
    y = worker // 2
    return 2 * (y + upper_half * (7 - 2 * y)) + worker % 2


def low_row(worker):
    return TILE + low_home(worker) * (2 * LOW) + worker // 8 * LOW


def slots_kernel(
    corners, live, me, own_hbm, low_mine, low_other, probe_hbm, pattern_hbm, left_hbm, right_hbm,
    keep_own, send_own, keep_low, send_low,
    cells, sums, wave, half, probe, pattern, left, right, sem,
):
    core = me[0] % 2
    pairs = [(own_hbm, cells.at[0:TILE]), (probe_hbm, probe), (left_hbm, left), (right_hbm, right),
             (pattern_hbm, pattern)]
    for y in range(WORKERS // 2):
        mine = pl.multiple_of(low_row(2 * y + core), LOW)
        other = pl.multiple_of(low_row(2 * y + 1 - core), LOW)
        pairs.append((low_mine.at[y], cells.at[pl.ds(mine, LOW)]))
        pairs.append((low_other.at[y], cells.at[pl.ds(other, LOW)]))
    fetches = [pltpu.make_async_copy(source, target, sem.at[i]) for i, (source, target) in enumerate(pairs)]
    for copy in fetches:
        copy.start()

    def clear(i, _):
        sums[pl.ds(pl.multiple_of(i * 16, 16), 16), :] = jnp.zeros((16, 2 * WIDE), jnp.float32)
        return 0

    lax.fori_loop(0, WIDE // 16, clear, 0)
    for copy in fetches:
        copy.wait()

    def one(slot, _):
        row = corners[slot, 0]
        col = corners[slot, 1]
        base = pl.multiple_of(col // 128 * 128, 128)
        shift = col % 128
        back = (SPAN - shift) % SPAN
        for i in range(4):
            here = slice(64 * i, 64 * i + 64)
            rows = pl.ds(pl.multiple_of(row + 64 * i, 8), 64)
            cell_re = pltpu.roll(cells[rows, pl.ds(base, SPAN)], back, 1)[:, :SIDE]
            cell_im = pltpu.roll(cells[rows, pl.ds(pl.multiple_of(base + WIDE, 128), SPAN)], back, 1)[:, :SIDE]
            probe_re = probe[0, here, :]
            probe_im = probe[1, here, :]
            wave[here, :] = (probe_re * cell_re - probe_im * cell_im).astype(jnp.bfloat16)
            wave[64 * i + SIDE:64 * i + SIDE + 64, :] = (
                probe_re * cell_im + probe_im * cell_re).astype(jnp.bfloat16)
        half_way = jnp.dot(left[...], wave[...], preferred_element_type=jnp.float32).astype(jnp.bfloat16)
        half[:, :SIDE] = half_way[:SIDE]
        half[:, SIDE:] = half_way[SIDE:]
        far = jnp.dot(half[...], right[...], preferred_element_type=jnp.float32)
        far_re = far[:, :SIDE]
        far_im = far[:, SIDE:]
        ratio = pattern[slot].astype(jnp.float32) * lax.rsqrt(far_re * far_re + far_im * far_im + 0.01)
        half[:, :SIDE] = (far_re * ratio).astype(jnp.bfloat16)
        half[:, SIDE:] = (far_im * ratio).astype(jnp.bfloat16)
        half_back = jnp.dot(half[...], left[...], preferred_element_type=jnp.float32).astype(jnp.bfloat16)
        wave[:SIDE, :] = half_back[:, :SIDE]
        wave[SIDE:, :] = half_back[:, SIDE:]
        near = jnp.dot(right[...], wave[...], preferred_element_type=jnp.float32)
        for i in range(4):
            here = slice(64 * i, 64 * i + 64)
            rows = pl.ds(pl.multiple_of(row + 64 * i, 8), 64)
            near_re = near[64 * i:64 * i + 64]
            near_im = near[64 * i + SIDE:64 * i + SIDE + 64]
            probe_re = probe[0, here, :]
            probe_im = probe[1, here, :]
            blank = jnp.zeros((64, 128), jnp.float32)
            term_re = jnp.concatenate([probe_re * near_re + probe_im * near_im, blank], 1)
            term_im = jnp.concatenate([probe_re * near_im - probe_im * near_re, blank], 1)
            sums[rows, pl.ds(base, SPAN)] += pltpu.roll(term_re, shift, 1)
            sums[rows, pl.ds(pl.multiple_of(base + WIDE, 128), SPAN)] += pltpu.roll(term_im, shift, 1)
        return 0

    lax.fori_loop(0, live[0, 0], one, 0)

    copies = []
    for y in range(WORKERS // 2):
        mine = pl.multiple_of(low_row(2 * y + core), LOW)
        other = pl.multiple_of(low_row(2 * y + 1 - core), LOW)
        own_mine = pl.multiple_of((2 * y + core) * OWN, OWN)
        own_other = pl.multiple_of((2 * y + 1 - core) * OWN, OWN)
        copies.append(pltpu.make_async_copy(sums.at[pl.ds(other, LOW)], send_low.at[y], sem.at[4 * y]))
        copies.append(pltpu.make_async_copy(sums.at[pl.ds(mine, LOW)], keep_low.at[y], sem.at[4 * y + 1]))
        copies.append(pltpu.make_async_copy(sums.at[pl.ds(own_other, OWN)], send_own.at[y], sem.at[4 * y + 2]))
        copies.append(pltpu.make_async_copy(sums.at[pl.ds(own_mine, OWN)], keep_own.at[y], sem.at[4 * y + 3]))
    for copy in copies:
        copy.start()
    for copy in copies:
        copy.wait()


def weight_kernel(corners, live, me, probe, weights, padded):
    padded[...] = jnp.zeros_like(padded)
    for i in range(4):
        here = slice(64 * i, 64 * i + 64)
        probe_re = probe[0, here, :]
        probe_im = probe[1, here, :]
        padded[PAD + 64 * i:PAD + 64 * i + 64, 0:SIDE] = probe_re * probe_re + probe_im * probe_im
    weights[...] = jnp.zeros_like(weights)
    worker = me[0]
    own_first = worker * OWN
    low_first = low_row(worker)

    def one(index, _):
        other = index // SLOTS
        slot = index % SLOTS
        row = corners[other, 2 * slot]
        used = slot < live[other]
        col = jnp.where(used, corners[other, 2 * slot + 1], 0)
        base = pl.multiple_of(col // 128 * 128, 128)
        shift = col % 128

        def part(first, count, at):
            start = jnp.where(used, jnp.clip(first - row + PAD, 0, PAD + SIDE), 0)
            piece = padded[pl.ds(pl.multiple_of(start, 8), count), :]
            weights[at:at + count, pl.ds(base, SPAN)] += pltpu.roll(piece, shift, 1)

        part(own_first, OWN, 0)
        part(low_first, LOW, OWN)
        return 0

    lax.fori_loop(0, WORKERS * SLOTS, one, 0)


def smem():
    return pl.BlockSpec(memory_space=pltpu.SMEM)


def vmem():
    return pl.BlockSpec(memory_space=pltpu.VMEM)


def hbm():
    return pl.BlockSpec(memory_space=pl.ANY)


def patch_sums(corners, live, me, own_cells, low_mine, low_other, probe, patterns, left, right):
    own_chunk = jax.ShapeDtypeStruct((WORKERS // 2, OWN, 2 * WIDE), jnp.float32)
    low_chunk = jax.ShapeDtypeStruct((WORKERS // 2, LOW, 2 * WIDE), jnp.float32)
    return pl.pallas_call(
        slots_kernel,
        out_shape=(own_chunk, own_chunk, low_chunk, low_chunk),
        in_specs=[smem()] * 3 + [hbm()] * 7,
        out_specs=(hbm(), hbm(), hbm(), hbm()),
        scratch_shapes=[
            pltpu.VMEM((WIDE, 2 * WIDE), jnp.float32),
            pltpu.VMEM((WIDE, 2 * WIDE), jnp.float32),
            pltpu.VMEM((2 * SIDE, SIDE), jnp.bfloat16),
            pltpu.VMEM((SIDE, 2 * SIDE), jnp.bfloat16),
            pltpu.VMEM((2, SIDE, SIDE), jnp.float32),
            pltpu.VMEM((SLOTS, SIDE, SIDE), jnp.bfloat16),
            pltpu.VMEM((2 * SIDE, 2 * SIDE), jnp.bfloat16),
            pltpu.VMEM((2 * SIDE, 2 * SIDE), jnp.bfloat16),
            pltpu.SemaphoreType.DMA((5 + 2 * WORKERS,)),
        ],
        compiler_params=pltpu.CompilerParams(vmem_limit_bytes=61 * 2**20),
        cost_estimate=pl.CostEstimate(flops=2 * 10**9, bytes_accessed=12 * 10**6, transcendentals=0),
        name="patch_sums",
    )(corners, live, me, own_cells, low_mine, low_other, probe, patterns, left, right)


def weight_rows(corners, live, me, probe):
    return pl.pallas_call(
        weight_kernel,
        out_shape=jax.ShapeDtypeStruct((ROWS, WIDE), jnp.float32),
        in_specs=[smem(), smem(), smem(), vmem()],
        out_specs=vmem(),
        scratch_shapes=[pltpu.VMEM((SIDE + 2 * PAD, SPAN), jnp.float32)],
        compiler_params=pltpu.CompilerParams(vmem_limit_bytes=16 * 2**20),
        cost_estimate=pl.CostEstimate(flops=10**7, bytes_accessed=10**6, transcendentals=0),
        name="weight_rows",
    )(corners, live, me, probe)


def moved(value, tile_step, pick):
    pairs = []
    for tile in range(TILES):
        for worker in range(WORKERS):
            target = pick(tile, worker)
            if target is not None and 0 <= tile + tile_step < TILES:
                pairs.append((tile * WORKERS + worker, (tile + tile_step) * WORKERS + target))
    return lax.ppermute(value, ("obj", "pat"), pairs)


def local(obj_tiles, probe_wave, amplitudes, offsets, live_count):
    own = obj_tiles[0]
    me = lax.axis_index("pat").astype(jnp.int32)
    corners = offsets[0, 0]

    mirrored = lambda worker: 2 * (7 - worker // 2) + worker % 2
    first_half = lambda tile, worker: worker if worker < 8 else None
    second_half = lambda tile, worker: mirrored(worker) if worker < 8 else None
    mirrored = lambda worker: 2 * (7 - worker // 2) + worker % 2
    first_half = lambda tile, worker: worker if worker < 8 else None
    second_half = lambda tile, worker: mirrored(worker) if worker < 8 else None
    own_left = jnp.concatenate([own[0, :, :SIDE], own[1, :, :SIDE]], 1)
    from_right = moved(own_left, -1, lambda tile, worker: worker if tile % GRID_C else None)
    spare_re = jnp.zeros((OWN, 8), jnp.float32)
    spare_re = spare_re.at[0].set(corners.reshape(8).astype(jnp.float32))
    spare_re = spare_re.at[1].set(jnp.broadcast_to(live_count[0, 0].astype(jnp.float32), (8,)))
    shard = jnp.concatenate(
        [own[0], from_right[:, :SIDE - 8], spare_re, own[1], from_right[:, SIDE:]], 1)
    own_cells = lax.all_gather(shard, "pat", axis=0, tiled=True)
    low = moved(shard[:LOW], -GRID_C, first_half) + moved(shard[LOW:], -GRID_C, second_half)
    same_core = [list(range(0, WORKERS, 2)), list(range(1, WORKERS, 2))]
    sibling = [(i, i ^ 1) for i in range(WORKERS)]

    low_mine = lax.all_gather(low, "pat", axis=0, tiled=True, axis_index_groups=same_core)
    low_mine = low_mine.reshape(WORKERS // 2, LOW, 2 * WIDE)
    low_other = lax.ppermute(low_mine, "pat", sibling)

    left_table, right_table = dft_blocks(SIDE)
    keep_own, send_own, keep_low, send_low = patch_sums(
        corners, live_count, me.reshape(1), own_cells, low_mine, low_other, probe_wave, amplitudes[0, 0],
        left_table, right_table)
    other_low = lax.ppermute(send_low, "pat", sibling)
    other_own = lax.ppermute(send_own, "pat", sibling)
    both_own = (keep_own + other_own).reshape(WORKERS // 2 * OWN, 2 * WIDE)
    both_low = keep_low + other_low
    both_own, both_low = lax.optimization_barrier((both_own, both_low))
    summed_own = lax.psum_scatter(
        both_own, "pat", scatter_dimension=0, tiled=True, axis_index_groups=same_core)

    by_tile = own_cells.reshape(WORKERS, OWN, 2 * WIDE)
    tile_corners = by_tile[:, 0, WIDE - 8:WIDE].astype(jnp.int32)
    tile_live = by_tile[:, 1, WIDE - 8].astype(jnp.int32)
    weights = weight_rows(tile_corners, tile_live, me.reshape(1), probe_wave)

    summed_low = jnp.sum(lax.all_to_all(both_low, "pat", 0, 0, axis_index_groups=same_core), 0)
    low_sums = jnp.concatenate([summed_low, weights[OWN:]], 1)
    down_first = moved(low_sums, GRID_C, first_half)
    down_second = moved(low_sums, GRID_C, lambda tile, worker: mirrored(worker) if worker >= 8 else None)
    upper_sum = (
        jnp.concatenate([summed_own, weights[:OWN]], 1) + jnp.concatenate([down_first, down_second], 0)
    ).reshape(OWN, 3, WIDE)
    to_right = upper_sum[:, :, TILE:].reshape(OWN, 3 * SIDE)
    from_left = moved(to_right, 1, lambda tile, worker: worker if tile % GRID_C != GRID_C - 1 else None)
    total = upper_sum[:, :, :TILE] + jnp.pad(
        from_left.reshape(OWN, 3, SIDE), ((0, 0), (0, 0), (0, TILE - SIDE)))
    weight = total[:, 2]
    over = 1.0 / (weight + 1.0)
    return jnp.stack([
        (total[:, 0] - weight * own[0]) * over,
        (total[:, 1] - weight * own[1]) * over,
    ])[None]


def solution(mesh):
    in_specs = (
        P("obj", None, "pat", None),
        P(),
        P("obj", "pat", None, None, None),
        P("obj", "pat", None, None),
        P("obj", "pat"),
    )
    out_specs = P("obj", None, "pat", None)
    return jax.shard_map(local, mesh=mesh, in_specs=in_specs, out_specs=out_specs, check_vma=False)
```

```python
import jax
import jax.numpy as jnp
import numpy as np
from jax import lax
from jax.experimental import pallas as pl
from jax.experimental.pallas import tpu as pltpu
from jax.sharding import PartitionSpec as P

GRID_C = 4
TILES = 32
WORKERS = 16
SLOTS = 4
SIDE = 256
TILE = 512
WIDE = TILE + SIDE
OWN = TILE // WORKERS
LOW = SIDE // WORKERS
ROWS = OWN + LOW
SPAN = SIDE + 128
PAD = 48


def dft_blocks(side_len):
    index_line = np.arange(side_len)
    products = index_line[:, None] * index_line[None, :] % side_len
    angles = (2.0 * np.pi / side_len) * products
    cos_part = np.cos(angles) / np.sqrt(side_len)
    sin_part = -np.sin(angles) / np.sqrt(side_len)
    left_table = np.block([[cos_part, -sin_part], [sin_part, cos_part]])
    right_table = np.block([[cos_part, sin_part], [-sin_part, cos_part]])
    return tuple(jnp.asarray(table.astype(np.float32).astype(jnp.bfloat16)) for table in (left_table, right_table))


def low_home(worker):
    upper_half = worker // 8
    y = worker // 2
    return 2 * (y + upper_half * (7 - 2 * y)) + worker % 2


def low_row(worker):
    return TILE + low_home(worker) * (2 * LOW) + worker // 8 * LOW


def slots_kernel(
    corners, live, me, own_hbm, low_mine, low_other, probe_hbm, pattern_hbm, left_hbm, right_hbm,
    keep_own, send_own, keep_low, send_low,
    cells, sums, wave, half, probe, pattern, left, right, sem,
):
    core = me[0] % 2
    pairs = [(own_hbm, cells.at[0:TILE]), (probe_hbm, probe), (left_hbm, left), (right_hbm, right),
             (pattern_hbm, pattern)]
    for y in range(WORKERS // 2):
        mine = pl.multiple_of(low_row(2 * y + core), LOW)
        other = pl.multiple_of(low_row(2 * y + 1 - core), LOW)
        pairs.append((low_mine.at[y], cells.at[pl.ds(mine, LOW)]))
        pairs.append((low_other.at[y], cells.at[pl.ds(other, LOW)]))
    fetches = [pltpu.make_async_copy(source, target, sem.at[i]) for i, (source, target) in enumerate(pairs)]
    for copy in fetches:
        copy.start()

    def clear(i, _):
        sums[pl.ds(pl.multiple_of(i * 16, 16), 16), :] = jnp.zeros((16, 2 * WIDE), jnp.float32)
        return 0

    lax.fori_loop(0, WIDE // 16, clear, 0)
    for copy in fetches:
        copy.wait()

    def one(pair, _):
        at = []
        for e in range(2):
            slot = 2 * pair + e
            used = slot < live[0, 0]
            row = jnp.where(used, corners[slot, 0], 0)
            col = jnp.where(used, corners[slot, 1], 0)
            base = pl.multiple_of(col // 128 * 128, 128)
            at.append((used, row, base, pl.multiple_of(base + WIDE, 128), col % 128))
        for e, (used, row, base_re, base_im, shift) in enumerate(at):
            back = (SPAN - shift) % SPAN
            columns = slice(SIDE * e, SIDE * e + SIDE)
            for i in range(4):
                here = slice(64 * i, 64 * i + 64)
                rows = pl.ds(pl.multiple_of(row + 64 * i, 8), 64)
                cell_re = pltpu.roll(cells[rows, pl.ds(base_re, SPAN)], back, 1)[:, :SIDE]
                cell_im = pltpu.roll(cells[rows, pl.ds(base_im, SPAN)], back, 1)[:, :SIDE]
                probe_re = probe[0, here, :]
                probe_im = probe[1, here, :]
                wave[here, columns] = (probe_re * cell_re - probe_im * cell_im).astype(jnp.bfloat16)
                wave[64 * i + SIDE:64 * i + SIDE + 64, columns] = (
                    probe_re * cell_im + probe_im * cell_re).astype(jnp.bfloat16)
        half_way = jnp.dot(left[...], wave[...], preferred_element_type=jnp.float32).astype(jnp.bfloat16)
        for e in range(2):
            half[SIDE * e:SIDE * e + SIDE, :SIDE] = half_way[:SIDE, SIDE * e:SIDE * e + SIDE]
            half[SIDE * e:SIDE * e + SIDE, SIDE:] = half_way[SIDE:, SIDE * e:SIDE * e + SIDE]
        far = jnp.dot(half[...], right[...], preferred_element_type=jnp.float32)
        far_re = far[:, :SIDE]
        far_im = far[:, SIDE:]
        amplitude = pattern[pl.ds(2 * pair, 2)].reshape(2 * SIDE, SIDE).astype(jnp.float32)
        ratio = amplitude * lax.rsqrt(far_re * far_re + far_im * far_im + 0.01)
        half[:, :SIDE] = (far_re * ratio).astype(jnp.bfloat16)
        half[:, SIDE:] = (far_im * ratio).astype(jnp.bfloat16)
        half_back = jnp.dot(half[...], left[...], preferred_element_type=jnp.float32).astype(jnp.bfloat16)
        for e in range(2):
            wave[:SIDE, SIDE * e:SIDE * e + SIDE] = half_back[SIDE * e:SIDE * e + SIDE, :SIDE]
            wave[SIDE:, SIDE * e:SIDE * e + SIDE] = half_back[SIDE * e:SIDE * e + SIDE, SIDE:]
        near = jnp.dot(right[...], wave[...], preferred_element_type=jnp.float32)
        for e, (used, row, base_re, base_im, shift) in enumerate(at):
            columns = slice(SIDE * e, SIDE * e + SIDE)
            for i in range(4):
                here = slice(64 * i, 64 * i + 64)
                rows = pl.ds(pl.multiple_of(row + 64 * i, 8), 64)
                near_re = near[64 * i:64 * i + 64, columns]
                near_im = near[64 * i + SIDE:64 * i + SIDE + 64, columns]
                probe_re = probe[0, here, :]
                probe_im = probe[1, here, :]
                blank = jnp.zeros((64, 128), jnp.float32)
                term_re = jnp.where(used, probe_re * near_re + probe_im * near_im, 0.0)
                term_im = jnp.where(used, probe_re * near_im - probe_im * near_re, 0.0)
                sums[rows, pl.ds(base_re, SPAN)] += pltpu.roll(jnp.concatenate([term_re, blank], 1), shift, 1)
                sums[rows, pl.ds(base_im, SPAN)] += pltpu.roll(jnp.concatenate([term_im, blank], 1), shift, 1)
        return 0

    lax.fori_loop(0, (live[0, 0] + 1) // 2, one, 0)

    copies = []
    for y in range(WORKERS // 2):
        mine = pl.multiple_of(low_row(2 * y + core), LOW)
        other = pl.multiple_of(low_row(2 * y + 1 - core), LOW)
        own_mine = pl.multiple_of((2 * y + core) * OWN, OWN)
        own_other = pl.multiple_of((2 * y + 1 - core) * OWN, OWN)
        copies.append(pltpu.make_async_copy(sums.at[pl.ds(other, LOW)], send_low.at[y], sem.at[4 * y]))
        copies.append(pltpu.make_async_copy(sums.at[pl.ds(mine, LOW)], keep_low.at[y], sem.at[4 * y + 1]))
        copies.append(pltpu.make_async_copy(sums.at[pl.ds(own_other, OWN)], send_own.at[y], sem.at[4 * y + 2]))
        copies.append(pltpu.make_async_copy(sums.at[pl.ds(own_mine, OWN)], keep_own.at[y], sem.at[4 * y + 3]))
    for copy in copies:
        copy.start()
    for copy in copies:
        copy.wait()


def weight_kernel(corners, live, me, probe, weights, padded):
    padded[...] = jnp.zeros_like(padded)
    for i in range(4):
        here = slice(64 * i, 64 * i + 64)
        probe_re = probe[0, here, :]
        probe_im = probe[1, here, :]
        padded[PAD + 64 * i:PAD + 64 * i + 64, 0:SIDE] = probe_re * probe_re + probe_im * probe_im
    weights[...] = jnp.zeros_like(weights)
    own_first = me[0] * OWN

    def one(index, _):
        source = index // SLOTS
        slot = index % SLOTS
        used = slot < live[source]
        row = corners[source, 2 * slot] - jnp.where(source < WORKERS, 0, TILE)
        col = corners[source, 2 * slot + 1]
        first = own_first - row

        @pl.when(used & (first > -OWN) & (first < SIDE))
        def _():
            base = pl.multiple_of(col // 128 * 128, 128)
            piece = padded[pl.ds(pl.multiple_of(first + PAD, 8), OWN), :]
            weights[:, pl.ds(base, SPAN)] += pltpu.roll(piece, col % 128, 1)

        return 0

    lax.fori_loop(0, 2 * WORKERS * SLOTS, one, 0)


def smem():
    return pl.BlockSpec(memory_space=pltpu.SMEM)


def vmem():
    return pl.BlockSpec(memory_space=pltpu.VMEM)


def hbm():
    return pl.BlockSpec(memory_space=pl.ANY)


def patch_sums(corners, live, me, own_cells, low_mine, low_other, probe, patterns, left, right):
    own_chunk = jax.ShapeDtypeStruct((WORKERS // 2, OWN, 2 * WIDE), jnp.float32)
    low_chunk = jax.ShapeDtypeStruct((WORKERS // 2, LOW, 2 * WIDE), jnp.float32)
    return pl.pallas_call(
        slots_kernel,
        out_shape=(own_chunk, own_chunk, low_chunk, low_chunk),
        in_specs=[smem()] * 3 + [hbm()] * 7,
        out_specs=(hbm(), hbm(), hbm(), hbm()),
        scratch_shapes=[
            pltpu.VMEM((WIDE, 2 * WIDE), jnp.float32),
            pltpu.VMEM((WIDE, 2 * WIDE), jnp.float32),
            pltpu.VMEM((2 * SIDE, 2 * SIDE), jnp.bfloat16),
            pltpu.VMEM((2 * SIDE, 2 * SIDE), jnp.bfloat16),
            pltpu.VMEM((2, SIDE, SIDE), jnp.float32),
            pltpu.VMEM((SLOTS, SIDE, SIDE), jnp.bfloat16),
            pltpu.VMEM((2 * SIDE, 2 * SIDE), jnp.bfloat16),
            pltpu.VMEM((2 * SIDE, 2 * SIDE), jnp.bfloat16),
            pltpu.SemaphoreType.DMA((5 + 2 * WORKERS,)),
        ],
        compiler_params=pltpu.CompilerParams(vmem_limit_bytes=61 * 2**20),
        cost_estimate=pl.CostEstimate(flops=2 * 10**9, bytes_accessed=12 * 10**6, transcendentals=0),
        name="patch_sums",
    )(corners, live, me, own_cells, low_mine, low_other, probe, patterns, left, right)


def weight_rows(corners, live, me, probe):
    return pl.pallas_call(
        weight_kernel,
        out_shape=jax.ShapeDtypeStruct((OWN, WIDE), jnp.float32),
        in_specs=[smem(), smem(), smem(), vmem()],
        out_specs=vmem(),
        scratch_shapes=[pltpu.VMEM((SIDE + 2 * PAD, SPAN), jnp.float32)],
        compiler_params=pltpu.CompilerParams(vmem_limit_bytes=16 * 2**20),
        cost_estimate=pl.CostEstimate(flops=10**7, bytes_accessed=10**6, transcendentals=0),
        name="weight_rows",
    )(corners, live, me, probe)


def moved(value, tile_step, pick):
    pairs = []
    for tile in range(TILES):
        for worker in range(WORKERS):
            target = pick(tile, worker)
            if target is not None and 0 <= tile + tile_step < TILES:
                pairs.append((tile * WORKERS + worker, (tile + tile_step) * WORKERS + target))
    return lax.ppermute(value, ("obj", "pat"), pairs)


def local(obj_tiles, probe_wave, amplitudes, offsets, live_count):
    own = obj_tiles[0]
    me = lax.axis_index("pat").astype(jnp.int32)
    corners = offsets[0, 0]

    mirrored = lambda worker: 2 * (7 - worker // 2) + worker % 2
    first_half = lambda tile, worker: worker if worker < 8 else None
    second_half = lambda tile, worker: mirrored(worker) if worker < 8 else None
    own_left = jnp.concatenate([own[0, :, :SIDE], own[1, :, :SIDE]], 1)
    from_right = moved(own_left, -1, lambda tile, worker: worker if tile % GRID_C else None)
    spare_re = jnp.zeros((OWN, 8), jnp.float32)
    spare_re = spare_re.at[0].set(corners.reshape(8).astype(jnp.float32))
    spare_re = spare_re.at[1].set(jnp.broadcast_to(live_count[0, 0].astype(jnp.float32), (8,)))
    shard = jnp.concatenate(
        [own[0], from_right[:, :SIDE - 8], spare_re, own[1], from_right[:, SIDE:]], 1)
    own_cells = lax.all_gather(shard, "pat", axis=0, tiled=True)
    low = moved(shard[:LOW], -GRID_C, first_half) + moved(shard[LOW:], -GRID_C, second_half)
    same_core = [list(range(0, WORKERS, 2)), list(range(1, WORKERS, 2))]
    sibling = [(i, i ^ 1) for i in range(WORKERS)]

    low_mine = lax.all_gather(low, "pat", axis=0, tiled=True, axis_index_groups=same_core)
    low_mine = low_mine.reshape(WORKERS // 2, LOW, 2 * WIDE)
    low_other = lax.ppermute(low_mine, "pat", sibling)

    left_table, right_table = dft_blocks(SIDE)
    keep_own, send_own, keep_low, send_low = patch_sums(
        corners, live_count, me.reshape(1), own_cells, low_mine, low_other, probe_wave, amplitudes[0, 0],
        left_table, right_table)
    other_low = lax.ppermute(send_low, "pat", sibling)
    other_own = lax.ppermute(send_own, "pat", sibling)
    both_own = (keep_own + other_own).reshape(WORKERS // 2 * OWN, 2 * WIDE)
    both_low = keep_low + other_low
    marks = own_cells.reshape(WORKERS, OWN, 2 * WIDE)[:, :2, WIDE - 8:WIDE].reshape(WORKERS, 16)
    both_own, both_low, marks = lax.optimization_barrier((both_own, both_low, marks))
    summed_own = lax.psum_scatter(
        both_own, "pat", scatter_dimension=0, tiled=True, axis_index_groups=same_core)

    upper_marks = moved(jnp.pad(marks, ((0, 0), (0, 112))), GRID_C, lambda tile, worker: worker)
    all_marks = jnp.concatenate([marks, upper_marks[:, :16]], 0).astype(jnp.int32)
    weights = weight_rows(all_marks[:, :8], all_marks[:, 8], me.reshape(1), probe_wave)

    summed_low = jnp.sum(lax.all_to_all(both_low, "pat", 0, 0, axis_index_groups=same_core), 0)

    def main_columns(rows, parts):
        return jnp.concatenate([rows[:, part * WIDE:part * WIDE + TILE] for part in range(parts)], 1)

    def right_columns(rows, parts):
        return jnp.concatenate([rows[:, part * WIDE + TILE:(part + 1) * WIDE] for part in range(parts)], 1)

    inside = lambda tile: tile % GRID_C != GRID_C - 1
    direct = lambda worker: worker if worker < 8 else None
    by_mirror = lambda worker: mirrored(worker) if worker >= 8 else None

    def pushed_down(rows, pick):
        below = moved(main_columns(rows, 2), GRID_C, lambda tile, worker: pick(worker))
        corner = moved(right_columns(rows, 2), GRID_C + 1, lambda tile, worker: pick(worker) if inside(tile) else None)
        return below, corner

    def with_side(here, side):
        parts = []
        for part in range(here.shape[1] // TILE):
            first, cut, last = part * TILE, part * TILE + SIDE, (part + 1) * TILE
            parts += [here[:, first:cut] + side[:, part * SIDE:(part + 1) * SIDE], here[:, cut:last]]
        return jnp.concatenate(parts, 1)

    from_mirror = pushed_down(summed_low, by_mirror)
    from_direct = pushed_down(summed_low, direct)
    own_sums = jnp.concatenate([summed_own, weights], 1)
    from_left = moved(right_columns(own_sums, 3), 1, lambda tile, worker: worker if inside(tile) else None)
    main = main_columns(own_sums, 3)
    lower, top = lax.optimization_barrier((with_side(main[LOW:, :2 * TILE] + from_mirror[0], from_mirror[1]), main[:LOW, :2 * TILE]))
    top, lower = lax.optimization_barrier((top + from_direct[0], lower))
    lower, top = lax.optimization_barrier((
        with_side(lower, from_left[LOW:, :2 * SIDE]), with_side(top, from_left[:LOW, :2 * SIDE])))
    weight = with_side(main[:, 2 * TILE:], from_left[:, 2 * SIDE:])
    main = jnp.concatenate([with_side(top, from_direct[1]), lower], 0)

    over = 1.0 / (weight + 1.0)
    total = lambda part: main[:, part * TILE:(part + 1) * TILE]
    return jnp.stack([(total(part) - weight * own[part]) * over for part in range(2)])[None]


def solution(mesh):
    in_specs = (
        P("obj", None, "pat", None),
        P(),
        P("obj", "pat", None, None, None),
        P("obj", "pat", None, None),
        P("obj", "pat"),
    )
    out_specs = P("obj", None, "pat", None)
    return jax.shard_map(local, mesh=mesh, in_specs=in_specs, out_specs=out_specs, check_vma=False)
```

```python
import jax
import jax.numpy as jnp
import numpy as np
from jax import lax
from jax.experimental import pallas as pl
from jax.experimental.pallas import tpu as pltpu
from jax.sharding import PartitionSpec as P

GRID_C = 4
TILES = 32
WORKERS = 16
SLOTS = 4
SIDE = 256
TILE = 512
WIDE = TILE + SIDE
OWN = TILE // WORKERS
LOW = SIDE // WORKERS
ROWS = OWN + LOW
SPAN = SIDE + 128
PAD = 48


def dft_blocks(side_len):
    index_line = np.arange(side_len)
    products = index_line[:, None] * index_line[None, :] % side_len
    angles = (2.0 * np.pi / side_len) * products
    cos_part = np.cos(angles) / np.sqrt(side_len)
    sin_part = -np.sin(angles) / np.sqrt(side_len)
    left_table = np.block([[cos_part, -sin_part], [sin_part, cos_part]])
    right_table = np.block([[cos_part, sin_part], [-sin_part, cos_part]])
    return tuple(jnp.asarray(table.astype(np.float32).astype(jnp.bfloat16)) for table in (left_table, right_table))


def low_home(worker):
    upper_half = worker // 8
    y = worker // 2
    return 2 * (y + upper_half * (7 - 2 * y)) + worker % 2


def low_row(worker):
    return TILE + low_home(worker) * (2 * LOW) + worker // 8 * LOW


def slots_kernel(
    corners, live, me, own_hbm, low_mine, low_other, probe_hbm, pattern_hbm, left_hbm, right_hbm,
    keep_own, send_own, keep_low, send_low,
    cells, sums, wave, half, probe, pattern, left, right, sem,
):
    core = me[0] % 2
    pairs = [(own_hbm, cells.at[0:TILE]), (probe_hbm, probe), (left_hbm, left), (right_hbm, right),
             (pattern_hbm, pattern)]
    for y in range(WORKERS // 2):
        mine = pl.multiple_of(low_row(2 * y + core), LOW)
        other = pl.multiple_of(low_row(2 * y + 1 - core), LOW)
        pairs.append((low_mine.at[y], cells.at[pl.ds(mine, LOW)]))
        pairs.append((low_other.at[y], cells.at[pl.ds(other, LOW)]))
    fetches = [pltpu.make_async_copy(source, target, sem.at[i]) for i, (source, target) in enumerate(pairs)]
    for copy in fetches:
        copy.start()

    def clear(i, _):
        sums[pl.ds(pl.multiple_of(i * 16, 16), 16), :] = jnp.zeros((16, 2 * WIDE), jnp.float32)
        return 0

    lax.fori_loop(0, WIDE // 16, clear, 0)
    for copy in fetches:
        copy.wait()

    def one(pair, _):
        at = []
        for e in range(2):
            slot = 2 * pair + e
            used = slot < live[0, 0]
            row = jnp.where(used, corners[slot, 0], 0)
            col = jnp.where(used, corners[slot, 1], 0)
            base = pl.multiple_of(col // 128 * 128, 128)
            at.append((used, row, base, pl.multiple_of(base + WIDE, 128), col % 128))
        for e, (used, row, base_re, base_im, shift) in enumerate(at):
            back = (SPAN - shift) % SPAN
            columns = slice(SIDE * e, SIDE * e + SIDE)
            for i in range(4):
                here = slice(64 * i, 64 * i + 64)
                rows = pl.ds(pl.multiple_of(row + 64 * i, 8), 64)
                cell_re = pltpu.roll(cells[rows, pl.ds(base_re, SPAN)], back, 1)[:, :SIDE]
                cell_im = pltpu.roll(cells[rows, pl.ds(base_im, SPAN)], back, 1)[:, :SIDE]
                probe_re = probe[0, here, :]
                probe_im = probe[1, here, :]
                wave[here, columns] = (probe_re * cell_re - probe_im * cell_im).astype(jnp.bfloat16)
                wave[64 * i + SIDE:64 * i + SIDE + 64, columns] = (
                    probe_re * cell_im + probe_im * cell_re).astype(jnp.bfloat16)
        half_way = jnp.dot(left[...], wave[...], preferred_element_type=jnp.float32).astype(jnp.bfloat16)
        for e in range(2):
            half[SIDE * e:SIDE * e + SIDE, :SIDE] = half_way[:SIDE, SIDE * e:SIDE * e + SIDE]
            half[SIDE * e:SIDE * e + SIDE, SIDE:] = half_way[SIDE:, SIDE * e:SIDE * e + SIDE]
        far = jnp.dot(half[...], right[...], preferred_element_type=jnp.float32)
        far_re = far[:, :SIDE]
        far_im = far[:, SIDE:]
        amplitude = pattern[pl.ds(2 * pair, 2)].reshape(2 * SIDE, SIDE).astype(jnp.float32)
        ratio = amplitude * lax.rsqrt(far_re * far_re + far_im * far_im + 0.01)
        half[:, :SIDE] = (far_re * ratio).astype(jnp.bfloat16)
        half[:, SIDE:] = (far_im * ratio).astype(jnp.bfloat16)
        half_back = jnp.dot(half[...], left[...], preferred_element_type=jnp.float32).astype(jnp.bfloat16)
        for e in range(2):
            wave[:SIDE, SIDE * e:SIDE * e + SIDE] = half_back[SIDE * e:SIDE * e + SIDE, :SIDE]
            wave[SIDE:, SIDE * e:SIDE * e + SIDE] = half_back[SIDE * e:SIDE * e + SIDE, SIDE:]
        near = jnp.dot(right[...], wave[...], preferred_element_type=jnp.float32)
        for e, (used, row, base_re, base_im, shift) in enumerate(at):
            columns = slice(SIDE * e, SIDE * e + SIDE)
            for i in range(4):
                here = slice(64 * i, 64 * i + 64)
                rows = pl.ds(pl.multiple_of(row + 64 * i, 8), 64)
                near_re = near[64 * i:64 * i + 64, columns]
                near_im = near[64 * i + SIDE:64 * i + SIDE + 64, columns]
                probe_re = probe[0, here, :]
                probe_im = probe[1, here, :]
                blank = jnp.zeros((64, 128), jnp.float32)
                term_re = jnp.where(used, probe_re * near_re + probe_im * near_im, 0.0)
                term_im = jnp.where(used, probe_re * near_im - probe_im * near_re, 0.0)
                sums[rows, pl.ds(base_re, SPAN)] += pltpu.roll(jnp.concatenate([term_re, blank], 1), shift, 1)
                sums[rows, pl.ds(base_im, SPAN)] += pltpu.roll(jnp.concatenate([term_im, blank], 1), shift, 1)
        return 0

    lax.fori_loop(0, (live[0, 0] + 1) // 2, one, 0)

    copies = []
    for y in range(WORKERS // 2):
        mine = pl.multiple_of(low_row(2 * y + core), LOW)
        other = pl.multiple_of(low_row(2 * y + 1 - core), LOW)
        own_mine = pl.multiple_of((2 * y + core) * OWN, OWN)
        own_other = pl.multiple_of((2 * y + 1 - core) * OWN, OWN)
        copies.append(pltpu.make_async_copy(sums.at[pl.ds(other, LOW)], send_low.at[y], sem.at[4 * y]))
        copies.append(pltpu.make_async_copy(sums.at[pl.ds(mine, LOW)], keep_low.at[y], sem.at[4 * y + 1]))
        copies.append(pltpu.make_async_copy(sums.at[pl.ds(own_other, OWN)], send_own.at[y], sem.at[4 * y + 2]))
        copies.append(pltpu.make_async_copy(sums.at[pl.ds(own_mine, OWN)], keep_own.at[y], sem.at[4 * y + 3]))
    for copy in copies:
        copy.start()
    for copy in copies:
        copy.wait()


def weight_kernel(corners, live, me, probe, weights, padded):
    padded[...] = jnp.zeros_like(padded)
    for i in range(4):
        here = slice(64 * i, 64 * i + 64)
        probe_re = probe[0, here, :]
        probe_im = probe[1, here, :]
        padded[PAD + 64 * i:PAD + 64 * i + 64, 0:SIDE] = probe_re * probe_re + probe_im * probe_im
    weights[...] = jnp.zeros_like(weights)
    own_first = me[0] * OWN

    def one(index, _):
        source = index // SLOTS
        slot = index % SLOTS
        used = slot < live[source]
        row = corners[source, 2 * slot] - jnp.where(source < WORKERS, 0, TILE)
        col = corners[source, 2 * slot + 1]
        first = own_first - row

        @pl.when(used & (first > -OWN) & (first < SIDE))
        def _():
            base = pl.multiple_of(col // 128 * 128, 128)
            piece = padded[pl.ds(pl.multiple_of(first + PAD, 8), OWN), :]
            weights[:, pl.ds(base, SPAN)] += pltpu.roll(piece, col % 128, 1)

        return 0

    lax.fori_loop(0, 2 * WORKERS * SLOTS, one, 0)


def low_kernel(parts, mirror_main, mirror_right, direct_main, direct_right):
    total = parts[0]
    for y in range(1, WORKERS // 2):
        total = total + parts[y]
    for main, right in ((mirror_main, mirror_right), (direct_main, direct_right)):
        main[:, :TILE] = total[:, :TILE]
        main[:, TILE:] = total[:, WIDE:WIDE + TILE]
        right[:, :SIDE] = total[:, TILE:WIDE]
        right[:, SIDE:] = total[:, WIDE + TILE:]


def smem():
    return pl.BlockSpec(memory_space=pltpu.SMEM)


def vmem():
    return pl.BlockSpec(memory_space=pltpu.VMEM)


def hbm():
    return pl.BlockSpec(memory_space=pl.ANY)


def patch_sums(corners, live, me, own_cells, low_mine, low_other, probe, patterns, left, right):
    own_chunk = jax.ShapeDtypeStruct((WORKERS // 2, OWN, 2 * WIDE), jnp.float32)
    low_chunk = jax.ShapeDtypeStruct((WORKERS // 2, LOW, 2 * WIDE), jnp.float32)
    return pl.pallas_call(
        slots_kernel,
        out_shape=(own_chunk, own_chunk, low_chunk, low_chunk),
        in_specs=[smem()] * 3 + [hbm()] * 7,
        out_specs=(hbm(), hbm(), hbm(), hbm()),
        scratch_shapes=[
            pltpu.VMEM((WIDE, 2 * WIDE), jnp.float32),
            pltpu.VMEM((WIDE, 2 * WIDE), jnp.float32),
            pltpu.VMEM((2 * SIDE, 2 * SIDE), jnp.bfloat16),
            pltpu.VMEM((2 * SIDE, 2 * SIDE), jnp.bfloat16),
            pltpu.VMEM((2, SIDE, SIDE), jnp.float32),
            pltpu.VMEM((SLOTS, SIDE, SIDE), jnp.bfloat16),
            pltpu.VMEM((2 * SIDE, 2 * SIDE), jnp.bfloat16),
            pltpu.VMEM((2 * SIDE, 2 * SIDE), jnp.bfloat16),
            pltpu.SemaphoreType.DMA((5 + 2 * WORKERS,)),
        ],
        compiler_params=pltpu.CompilerParams(vmem_limit_bytes=61 * 2**20),
        cost_estimate=pl.CostEstimate(flops=2 * 10**9, bytes_accessed=12 * 10**6, transcendentals=0),
        name="patch_sums",
    )(corners, live, me, own_cells, low_mine, low_other, probe, patterns, left, right)


def weight_rows(corners, live, me, probe):
    return pl.pallas_call(
        weight_kernel,
        out_shape=jax.ShapeDtypeStruct((OWN, WIDE), jnp.float32),
        in_specs=[smem(), smem(), smem(), vmem()],
        out_specs=vmem(),
        scratch_shapes=[pltpu.VMEM((SIDE + 2 * PAD, SPAN), jnp.float32)],
        compiler_params=pltpu.CompilerParams(vmem_limit_bytes=16 * 2**20),
        cost_estimate=pl.CostEstimate(flops=10**7, bytes_accessed=10**6, transcendentals=0),
        name="weight_rows",
    )(corners, live, me, probe)


def low_sums(parts):
    return pl.pallas_call(
        low_kernel,
        out_shape=(
            jax.ShapeDtypeStruct((LOW, 2 * TILE), jnp.float32), jax.ShapeDtypeStruct((LOW, 2 * SIDE), jnp.float32)) * 2,
        in_specs=[vmem()],
        out_specs=(vmem(), vmem()) * 2,
        compiler_params=pltpu.CompilerParams(vmem_limit_bytes=8 * 2**20),
        cost_estimate=pl.CostEstimate(flops=2 * 10**5, bytes_accessed=10**6, transcendentals=0),
        name="low_sums",
    )(parts)


def moved(value, tile_step, pick):
    pairs = []
    for tile in range(TILES):
        for worker in range(WORKERS):
            target = pick(tile, worker)
            if target is not None and 0 <= tile + tile_step < TILES:
                pairs.append((tile * WORKERS + worker, (tile + tile_step) * WORKERS + target))
    return lax.ppermute(value, ("obj", "pat"), pairs)


def local(obj_tiles, probe_wave, amplitudes, offsets, live_count):
    own = obj_tiles[0]
    me = lax.axis_index("pat").astype(jnp.int32)
    corners = offsets[0, 0]

    mirrored = lambda worker: 2 * (7 - worker // 2) + worker % 2
    first_half = lambda tile, worker: worker if worker < 8 else None
    second_half = lambda tile, worker: mirrored(worker) if worker < 8 else None
    own_left = jnp.concatenate([own[0, :, :SIDE], own[1, :, :SIDE]], 1)
    from_right = moved(own_left, -1, lambda tile, worker: worker if tile % GRID_C else None)
    spare_re = jnp.zeros((OWN, 8), jnp.float32)
    spare_re = spare_re.at[0].set(corners.reshape(8).astype(jnp.float32))
    spare_re = spare_re.at[1].set(jnp.broadcast_to(live_count[0, 0].astype(jnp.float32), (8,)))
    shard = jnp.concatenate(
        [own[0], from_right[:, :SIDE - 8], spare_re, own[1], from_right[:, SIDE:]], 1)
    own_cells = lax.all_gather(shard, "pat", axis=0, tiled=True)
    low = moved(shard[:LOW], -GRID_C, first_half) + moved(shard[LOW:], -GRID_C, second_half)
    same_core = [list(range(0, WORKERS, 2)), list(range(1, WORKERS, 2))]
    sibling = [(i, i ^ 1) for i in range(WORKERS)]

    low_mine = lax.all_gather(low, "pat", axis=0, tiled=True, axis_index_groups=same_core)
    low_mine = low_mine.reshape(WORKERS // 2, LOW, 2 * WIDE)
    low_other = lax.ppermute(low_mine, "pat", sibling)

    left_table, right_table = dft_blocks(SIDE)
    keep_own, send_own, keep_low, send_low = patch_sums(
        corners, live_count, me.reshape(1), own_cells, low_mine, low_other, probe_wave, amplitudes[0, 0],
        left_table, right_table)
    other_low = lax.ppermute(send_low, "pat", sibling)
    other_own = lax.ppermute(send_own, "pat", sibling)
    both_own = (keep_own + other_own).reshape(WORKERS // 2 * OWN, 2 * WIDE)
    marks = own_cells.reshape(WORKERS, OWN, 2 * WIDE)[:, :2, WIDE - 8:WIDE].reshape(WORKERS, 16)
    both_own, other_low, marks = lax.optimization_barrier((both_own, other_low, marks))
    both_low = keep_low + other_low
    summed_own = lax.psum_scatter(
        both_own, "pat", scatter_dimension=0, tiled=True, axis_index_groups=same_core)

    upper_marks = moved(jnp.pad(marks, ((0, 0), (0, 112))), GRID_C, lambda tile, worker: worker)
    all_marks = jnp.concatenate([marks, upper_marks[:, :16]], 0).astype(jnp.int32)
    weights = weight_rows(all_marks[:, :8], all_marks[:, 8], me.reshape(1), probe_wave)

    mirror_main, mirror_right, direct_main, direct_right = low_sums(lax.all_to_all(both_low, "pat", 0, 0, axis_index_groups=same_core))

    def main_columns(rows, parts):
        return jnp.concatenate([rows[:, part * WIDE:part * WIDE + TILE] for part in range(parts)], 1)

    def right_columns(rows, parts):
        return jnp.concatenate([rows[:, part * WIDE + TILE:(part + 1) * WIDE] for part in range(parts)], 1)

    inside = lambda tile: tile % GRID_C != GRID_C - 1
    direct = lambda worker: worker if worker < 8 else None
    by_mirror = lambda worker: mirrored(worker) if worker >= 8 else None

    def pushed_down(main, right, pick):
        below = moved(main, GRID_C, lambda tile, worker: pick(worker))
        corner = moved(right, GRID_C + 1, lambda tile, worker: pick(worker) if inside(tile) else None)
        return below, corner

    def with_side(here, side):
        parts = []
        for part in range(here.shape[1] // TILE):
            first, cut, last = part * TILE, part * TILE + SIDE, (part + 1) * TILE
            parts += [here[:, first:cut] + side[:, part * SIDE:(part + 1) * SIDE], here[:, cut:last]]
        return jnp.concatenate(parts, 1)

    from_mirror = pushed_down(mirror_main, mirror_right, by_mirror)
    from_direct = pushed_down(direct_main, direct_right, direct)
    own_sums = jnp.concatenate([summed_own, weights], 1)
    from_left = moved(right_columns(own_sums, 3), 1, lambda tile, worker: worker if inside(tile) else None)
    main = main_columns(own_sums, 3)
    lower, top = lax.optimization_barrier((with_side(main[LOW:, :2 * TILE] + from_mirror[0], from_mirror[1]), main[:LOW, :2 * TILE]))
    top, lower = lax.optimization_barrier((top + from_direct[0], lower))
    lower, top = lax.optimization_barrier((
        with_side(lower, from_left[LOW:, :2 * SIDE]), with_side(top, from_left[:LOW, :2 * SIDE])))
    weight = with_side(main[:, 2 * TILE:], from_left[:, 2 * SIDE:])
    main = jnp.concatenate([with_side(top, from_direct[1]), lower], 0)

    over = 1.0 / (weight + 1.0)
    total = lambda part: main[:, part * TILE:(part + 1) * TILE]
    return jnp.stack([(total(part) - weight * own[part]) * over for part in range(2)])[None]


def solution(mesh):
    in_specs = (
        P("obj", None, "pat", None),
        P(),
        P("obj", "pat", None, None, None),
        P("obj", "pat", None, None),
        P("obj", "pat"),
    )
    out_specs = P("obj", None, "pat", None)
    return jax.shard_map(local, mesh=mesh, in_specs=in_specs, out_specs=out_specs, check_vma=False)
```

```python
import jax
import jax.numpy as jnp
import numpy as np
from jax import lax
from jax.experimental import pallas as pl
from jax.experimental.pallas import tpu as pltpu
from jax.sharding import PartitionSpec as P

GRID_C = 4
TILES = 32
WORKERS = 16
SLOTS = 4
SIDE = 256
TILE = 512
WIDE = TILE + SIDE
OWN = TILE // WORKERS
LOW = SIDE // WORKERS
ROWS = OWN + LOW
SPAN = SIDE + 128
PAD = 48


def dft_blocks(side_len):
    index_line = np.arange(side_len)
    products = index_line[:, None] * index_line[None, :] % side_len
    angles = (2.0 * np.pi / side_len) * products
    cos_part = np.cos(angles) / np.sqrt(side_len)
    sin_part = -np.sin(angles) / np.sqrt(side_len)
    left_table = np.block([[cos_part, -sin_part], [sin_part, cos_part]])
    right_table = np.block([[cos_part, sin_part], [-sin_part, cos_part]])
    return tuple(jnp.asarray(table.astype(np.float32).astype(jnp.bfloat16)) for table in (left_table, right_table))


def low_home(worker):
    upper_half = worker // 8
    y = worker // 2
    return 2 * (y + upper_half * (7 - 2 * y)) + worker % 2


def low_row(worker):
    return TILE + low_home(worker) * (2 * LOW) + worker // 8 * LOW


def slots_kernel(
    corners, live, me, own_hbm, low_mine, low_other, probe_hbm, pattern_hbm, left_hbm, right_hbm,
    keep_own, send_own, keep_low, send_low,
    cells, sums, wave, half, probe, pattern, left, right, sem,
):
    core = me[0] % 2
    pairs = [(own_hbm, cells.at[0:TILE]), (probe_hbm, probe)]
    for y in range(WORKERS // 2):
        mine = pl.multiple_of(low_row(2 * y + core), LOW)
        other = pl.multiple_of(low_row(2 * y + 1 - core), LOW)
        pairs.append((low_mine.at[y], cells.at[pl.ds(mine, LOW)]))
        pairs.append((low_other.at[y], cells.at[pl.ds(other, LOW)]))
    first_needs = len(pairs)
    pairs += [(left_hbm, left), (right_hbm, right), (pattern_hbm, pattern)]
    fetches = [pltpu.make_async_copy(source, target, sem.at[i]) for i, (source, target) in enumerate(pairs)]
    for copy in fetches:
        copy.start()

    def clear(i, _):
        sums[pl.ds(pl.multiple_of(i * 16, 16), 16), :] = jnp.zeros((16, 2 * WIDE), jnp.float32)
        return 0

    lax.fori_loop(0, WIDE // 16, clear, 0)
    for copy in fetches[:first_needs]:
        copy.wait()

    def place(slot):
        used = slot < live[0, 0]
        row = jnp.where(used, corners[slot, 0], 0)
        col = jnp.where(used, corners[slot, 1], 0)
        base = pl.multiple_of(col // 128 * 128, 128)
        return used, row, base, pl.multiple_of(base + WIDE, 128), col % 128

    def take(slot):
        _, row, base_re, base_im, shift = place(slot)
        back = (SPAN - shift) % SPAN
        columns = slice(SIDE * slot, SIDE * slot + SIDE)
        for i in range(4):
            here = slice(64 * i, 64 * i + 64)
            rows = pl.ds(pl.multiple_of(row + 64 * i, 8), 64)
            cell_re = pltpu.roll(cells[rows, pl.ds(base_re, SPAN)], back, 1)[:, :SIDE]
            cell_im = pltpu.roll(cells[rows, pl.ds(base_im, SPAN)], back, 1)[:, :SIDE]
            probe_re = probe[0, here, :]
            probe_im = probe[1, here, :]
            wave[here, columns] = (probe_re * cell_re - probe_im * cell_im).astype(jnp.bfloat16)
            wave[64 * i + SIDE:64 * i + SIDE + 64, columns] = (
                probe_re * cell_im + probe_im * cell_re).astype(jnp.bfloat16)

    def process(count):
        every = slice(0, SIDE * count)
        half_way = jnp.dot(left[...], wave[:, every], preferred_element_type=jnp.float32).astype(jnp.bfloat16)
        for e in range(count):
            columns = slice(SIDE * e, SIDE * e + SIDE)
            half[columns, :SIDE] = half_way[:SIDE, columns]
            half[columns, SIDE:] = half_way[SIDE:, columns]
        far = jnp.dot(half[every, :], right[...], preferred_element_type=jnp.float32)
        far_re = far[:, :SIDE]
        far_im = far[:, SIDE:]
        amplitude = pattern[0:count].reshape(count * SIDE, SIDE).astype(jnp.float32)
        ratio = amplitude * lax.rsqrt(far_re * far_re + far_im * far_im + 0.01)
        half[every, :SIDE] = (far_re * ratio).astype(jnp.bfloat16)
        half[every, SIDE:] = (far_im * ratio).astype(jnp.bfloat16)
        half_back = jnp.dot(half[every, :], left[...], preferred_element_type=jnp.float32).astype(jnp.bfloat16)
        for e in range(count):
            columns = slice(SIDE * e, SIDE * e + SIDE)
            wave[:SIDE, columns] = half_back[columns, :SIDE]
            wave[SIDE:, columns] = half_back[columns, SIDE:]
        near = jnp.dot(right[...], wave[:, every], preferred_element_type=jnp.float32)
        for e in range(count):
            used, row, base_re, base_im, shift = place(e)
            columns = slice(SIDE * e, SIDE * e + SIDE)
            for i in range(4):
                here = slice(64 * i, 64 * i + 64)
                rows = pl.ds(pl.multiple_of(row + 64 * i, 8), 64)
                near_re = near[64 * i:64 * i + 64, columns]
                near_im = near[64 * i + SIDE:64 * i + SIDE + 64, columns]
                probe_re = probe[0, here, :]
                probe_im = probe[1, here, :]
                blank = jnp.zeros((64, 128), jnp.float32)
                term_re = jnp.where(used, probe_re * near_re + probe_im * near_im, 0.0)
                term_im = jnp.where(used, probe_re * near_im - probe_im * near_re, 0.0)
                sums[rows, pl.ds(base_re, SPAN)] += pltpu.roll(jnp.concatenate([term_re, blank], 1), shift, 1)
                sums[rows, pl.ds(base_im, SPAN)] += pltpu.roll(jnp.concatenate([term_im, blank], 1), shift, 1)

    take(0)
    take(1)
    for copy in fetches[first_needs:]:
        copy.wait()

    @pl.when(live[0, 0] <= 2)
    def _():
        process(2)

    @pl.when(live[0, 0] > 2)
    def _():
        take(2)
        take(3)
        process(SLOTS)

    copies = []
    for y in range(WORKERS // 2):
        mine = pl.multiple_of(low_row(2 * y + core), LOW)
        other = pl.multiple_of(low_row(2 * y + 1 - core), LOW)
        own_mine = pl.multiple_of((2 * y + core) * OWN, OWN)
        own_other = pl.multiple_of((2 * y + 1 - core) * OWN, OWN)
        copies.append(pltpu.make_async_copy(sums.at[pl.ds(other, LOW)], send_low.at[y], sem.at[4 * y]))
        copies.append(pltpu.make_async_copy(sums.at[pl.ds(mine, LOW)], keep_low.at[y], sem.at[4 * y + 1]))
        copies.append(pltpu.make_async_copy(sums.at[pl.ds(own_other, OWN)], send_own.at[y], sem.at[4 * y + 2]))
        copies.append(pltpu.make_async_copy(sums.at[pl.ds(own_mine, OWN)], keep_own.at[y], sem.at[4 * y + 3]))
    for copy in copies:
        copy.start()
    for copy in copies:
        copy.wait()


def weight_kernel(corners, live, me, probe, weights, padded):
    padded[...] = jnp.zeros_like(padded)
    for i in range(4):
        here = slice(64 * i, 64 * i + 64)
        probe_re = probe[0, here, :]
        probe_im = probe[1, here, :]
        padded[PAD + 64 * i:PAD + 64 * i + 64, 0:SIDE] = probe_re * probe_re + probe_im * probe_im
    weights[...] = jnp.zeros_like(weights)
    own_first = me[0] * OWN

    def one(index, _):
        source = index // SLOTS
        slot = index % SLOTS
        used = slot < live[source]
        row = corners[source, 2 * slot] - jnp.where(source < WORKERS, 0, TILE)
        col = corners[source, 2 * slot + 1]
        first = own_first - row

        @pl.when(used & (first > -OWN) & (first < SIDE))
        def _():
            base = pl.multiple_of(col // 128 * 128, 128)
            piece = padded[pl.ds(pl.multiple_of(first + PAD, 8), OWN), :]
            weights[:, pl.ds(base, SPAN)] += pltpu.roll(piece, col % 128, 1)

        return 0

    lax.fori_loop(0, 2 * WORKERS * SLOTS, one, 0)


def low_kernel(parts, mirror_main, mirror_right, direct_main, direct_right):
    total = parts[0]
    for y in range(1, WORKERS // 2):
        total = total + parts[y]
    for main, right in ((mirror_main, mirror_right), (direct_main, direct_right)):
        main[:, :TILE] = total[:, :TILE]
        main[:, TILE:] = total[:, WIDE:WIDE + TILE]
        right[:, :SIDE] = total[:, TILE:WIDE]
        right[:, SIDE:] = total[:, WIDE + TILE:]


def smem():
    return pl.BlockSpec(memory_space=pltpu.SMEM)


def vmem():
    return pl.BlockSpec(memory_space=pltpu.VMEM)


def hbm():
    return pl.BlockSpec(memory_space=pl.ANY)


def patch_sums(corners, live, me, own_cells, low_mine, low_other, probe, patterns, left, right):
    own_chunk = jax.ShapeDtypeStruct((WORKERS // 2, OWN, 2 * WIDE), jnp.float32)
    low_chunk = jax.ShapeDtypeStruct((WORKERS // 2, LOW, 2 * WIDE), jnp.float32)
    return pl.pallas_call(
        slots_kernel,
        out_shape=(own_chunk, own_chunk, low_chunk, low_chunk),
        in_specs=[smem()] * 3 + [hbm()] * 7,
        out_specs=(hbm(), hbm(), hbm(), hbm()),
        scratch_shapes=[
            pltpu.VMEM((WIDE, 2 * WIDE), jnp.float32),
            pltpu.VMEM((WIDE, 2 * WIDE), jnp.float32),
            pltpu.VMEM((2 * SIDE, SLOTS * SIDE), jnp.bfloat16),
            pltpu.VMEM((SLOTS * SIDE, 2 * SIDE), jnp.bfloat16),
            pltpu.VMEM((2, SIDE, SIDE), jnp.float32),
            pltpu.VMEM((SLOTS, SIDE, SIDE), jnp.bfloat16),
            pltpu.VMEM((2 * SIDE, 2 * SIDE), jnp.bfloat16),
            pltpu.VMEM((2 * SIDE, 2 * SIDE), jnp.bfloat16),
            pltpu.SemaphoreType.DMA((5 + 2 * WORKERS,)),
        ],
        compiler_params=pltpu.CompilerParams(vmem_limit_bytes=61 * 2**20),
        cost_estimate=pl.CostEstimate(flops=2 * 10**9, bytes_accessed=12 * 10**6, transcendentals=0),
        name="patch_sums",
    )(corners, live, me, own_cells, low_mine, low_other, probe, patterns, left, right)


def weight_rows(corners, live, me, probe):
    return pl.pallas_call(
        weight_kernel,
        out_shape=jax.ShapeDtypeStruct((OWN, WIDE), jnp.float32),
        in_specs=[smem(), smem(), smem(), vmem()],
        out_specs=vmem(),
        scratch_shapes=[pltpu.VMEM((SIDE + 2 * PAD, SPAN), jnp.float32)],
        compiler_params=pltpu.CompilerParams(vmem_limit_bytes=16 * 2**20),
        cost_estimate=pl.CostEstimate(flops=10**7, bytes_accessed=10**6, transcendentals=0),
        name="weight_rows",
    )(corners, live, me, probe)


def low_sums(parts):
    return pl.pallas_call(
        low_kernel,
        out_shape=(
            jax.ShapeDtypeStruct((LOW, 2 * TILE), jnp.float32), jax.ShapeDtypeStruct((LOW, 2 * SIDE), jnp.float32)) * 2,
        in_specs=[vmem()],
        out_specs=(vmem(), vmem()) * 2,
        compiler_params=pltpu.CompilerParams(vmem_limit_bytes=8 * 2**20),
        cost_estimate=pl.CostEstimate(flops=2 * 10**5, bytes_accessed=10**6, transcendentals=0),
        name="low_sums",
    )(parts)


def moved(value, tile_step, pick):
    pairs = []
    for tile in range(TILES):
        for worker in range(WORKERS):
            target = pick(tile, worker)
            if target is not None and 0 <= tile + tile_step < TILES:
                pairs.append((tile * WORKERS + worker, (tile + tile_step) * WORKERS + target))
    return lax.ppermute(value, ("obj", "pat"), pairs)


def local(obj_tiles, probe_wave, amplitudes, offsets, live_count):
    own = obj_tiles[0]
    me = lax.axis_index("pat").astype(jnp.int32)
    corners = offsets[0, 0]

    mirrored = lambda worker: 2 * (7 - worker // 2) + worker % 2
    first_half = lambda tile, worker: worker if worker < 8 else None
    second_half = lambda tile, worker: mirrored(worker) if worker < 8 else None
    own_left = jnp.concatenate([own[0, :, :SIDE], own[1, :, :SIDE]], 1)
    from_right = moved(own_left, -1, lambda tile, worker: worker if tile % GRID_C else None)
    spare_re = jnp.zeros((OWN, 8), jnp.float32)
    spare_re = spare_re.at[0].set(corners.reshape(8).astype(jnp.float32))
    spare_re = spare_re.at[1].set(jnp.broadcast_to(live_count[0, 0].astype(jnp.float32), (8,)))
    shard = jnp.concatenate(
        [own[0], from_right[:, :SIDE - 8], spare_re, own[1], from_right[:, SIDE:]], 1)
    own_cells = lax.all_gather(shard, "pat", axis=0, tiled=True)
    low = moved(shard[:LOW], -GRID_C, first_half) + moved(shard[LOW:], -GRID_C, second_half)
    same_core = [list(range(0, WORKERS, 2)), list(range(1, WORKERS, 2))]
    sibling = [(i, i ^ 1) for i in range(WORKERS)]

    low_mine = lax.all_gather(low, "pat", axis=0, tiled=True, axis_index_groups=same_core)
    low_mine = low_mine.reshape(WORKERS // 2, LOW, 2 * WIDE)
    low_other = lax.ppermute(low_mine, "pat", sibling)

    left_table, right_table = dft_blocks(SIDE)
    keep_own, send_own, keep_low, send_low = patch_sums(
        corners, live_count, me.reshape(1), own_cells, low_mine, low_other, probe_wave, amplitudes[0, 0],
        left_table, right_table)
    other_low = lax.ppermute(send_low, "pat", sibling)
    other_own = lax.ppermute(send_own, "pat", sibling)
    both_own = (keep_own + other_own).reshape(WORKERS // 2 * OWN, 2 * WIDE)
    marks = own_cells.reshape(WORKERS, OWN, 2 * WIDE)[:, :2, WIDE - 8:WIDE].reshape(WORKERS, 16)
    both_own, other_low, marks = lax.optimization_barrier((both_own, other_low, marks))
    both_low = keep_low + other_low
    summed_own = lax.psum_scatter(
        both_own, "pat", scatter_dimension=0, tiled=True, axis_index_groups=same_core)

    upper_marks = moved(jnp.pad(marks, ((0, 0), (0, 112))), GRID_C, lambda tile, worker: worker)
    all_marks = jnp.concatenate([marks, upper_marks[:, :16]], 0).astype(jnp.int32)
    weights = weight_rows(all_marks[:, :8], all_marks[:, 8], me.reshape(1), probe_wave)

    mirror_main, mirror_right, direct_main, direct_right = low_sums(lax.all_to_all(both_low, "pat", 0, 0, axis_index_groups=same_core))

    def main_columns(rows, parts):
        return jnp.concatenate([rows[:, part * WIDE:part * WIDE + TILE] for part in range(parts)], 1)

    def right_columns(rows, parts):
        return jnp.concatenate([rows[:, part * WIDE + TILE:(part + 1) * WIDE] for part in range(parts)], 1)

    inside = lambda tile: tile % GRID_C != GRID_C - 1
    direct = lambda worker: worker if worker < 8 else None
    by_mirror = lambda worker: mirrored(worker) if worker >= 8 else None

    def pushed_down(main, right, pick):
        below = moved(main, GRID_C, lambda tile, worker: pick(worker))
        corner = moved(right, GRID_C + 1, lambda tile, worker: pick(worker) if inside(tile) else None)
        return below, corner

    def with_side(here, side):
        parts = []
        for part in range(here.shape[1] // TILE):
            first, cut, last = part * TILE, part * TILE + SIDE, (part + 1) * TILE
            parts += [here[:, first:cut] + side[:, part * SIDE:(part + 1) * SIDE], here[:, cut:last]]
        return jnp.concatenate(parts, 1)

    from_mirror = pushed_down(mirror_main, mirror_right, by_mirror)
    from_direct = pushed_down(direct_main, direct_right, direct)
    own_sums = jnp.concatenate([summed_own, weights], 1)
    from_left = moved(right_columns(own_sums, 3), 1, lambda tile, worker: worker if inside(tile) else None)
    main = main_columns(own_sums, 3)
    lower, top = lax.optimization_barrier((with_side(main[LOW:, :2 * TILE] + from_mirror[0], from_mirror[1]), main[:LOW, :2 * TILE]))
    top, lower = lax.optimization_barrier((top + from_direct[0], lower))
    lower, top = lax.optimization_barrier((
        with_side(lower, from_left[LOW:, :2 * SIDE]), with_side(top, from_left[:LOW, :2 * SIDE])))
    weight = with_side(main[:, 2 * TILE:], from_left[:, 2 * SIDE:])
    main = jnp.concatenate([with_side(top, from_direct[1]), lower], 0)

    over = 1.0 / (weight + 1.0)
    total = lambda part: main[:, part * TILE:(part + 1) * TILE]
    return jnp.stack([(total(part) - weight * own[part]) * over for part in range(2)])[None]


def solution(mesh):
    in_specs = (
        P("obj", None, "pat", None),
        P(),
        P("obj", "pat", None, None, None),
        P("obj", "pat", None, None),
        P("obj", "pat"),
    )
    out_specs = P("obj", None, "pat", None)
    return jax.shard_map(local, mesh=mesh, in_specs=in_specs, out_specs=out_specs, check_vma=False)
```

```python
import jax
import jax.numpy as jnp
import numpy as np
from jax import lax
from jax.experimental import pallas as pl
from jax.experimental.pallas import tpu as pltpu
from jax.sharding import PartitionSpec as P

GRID_C = 4
TILES = 32
WORKERS = 16
SLOTS = 4
SIDE = 256
TILE = 512
WIDE = TILE + SIDE
OWN = TILE // WORKERS
LOW = SIDE // WORKERS
ROWS = OWN + LOW
SPAN = SIDE + 128
PAD = 48


def dft_blocks(side_len):
    index_line = np.arange(side_len)
    products = index_line[:, None] * index_line[None, :] % side_len
    angles = (2.0 * np.pi / side_len) * products
    cos_part = np.cos(angles) / np.sqrt(side_len)
    sin_part = -np.sin(angles) / np.sqrt(side_len)
    left_table = np.block([[cos_part, -sin_part], [sin_part, cos_part]])
    right_table = np.block([[cos_part, sin_part], [-sin_part, cos_part]])
    return tuple(jnp.asarray(table.astype(np.float32).astype(jnp.bfloat16)) for table in (left_table, right_table))


def low_home(worker):
    upper_half = worker // 8
    y = worker // 2
    return 2 * (y + upper_half * (7 - 2 * y)) + worker % 2


def low_row(worker):
    return TILE + low_home(worker) * (2 * LOW) + worker // 8 * LOW


def slots_kernel(
    corners, live, me, own_hbm, low_mine, low_other, probe_hbm, pattern_hbm, left_hbm, right_hbm,
    keep_own, send_own, keep_low, send_low,
    cells, sums, wave, half, probe, pattern, left, right, sem,
):
    core = me[0] % 2
    pairs = [(own_hbm, cells.at[0:TILE]), (probe_hbm, probe)]
    for y in range(WORKERS // 2):
        mine = pl.multiple_of(low_row(2 * y + core), LOW)
        other = pl.multiple_of(low_row(2 * y + 1 - core), LOW)
        pairs.append((low_mine.at[y], cells.at[pl.ds(mine, LOW)]))
        pairs.append((low_other.at[y], cells.at[pl.ds(other, LOW)]))
    first_needs = len(pairs)
    pairs += [(left_hbm, left), (right_hbm, right), (pattern_hbm, pattern)]
    fetches = [pltpu.make_async_copy(source, target, sem.at[i]) for i, (source, target) in enumerate(pairs)]
    for copy in fetches:
        copy.start()

    def clear(i, _):
        sums[pl.ds(pl.multiple_of(i * 16, 16), 16), :] = jnp.zeros((16, 2 * WIDE), jnp.float32)
        return 0

    lax.fori_loop(0, WIDE // 16, clear, 0)
    for copy in fetches[:first_needs]:
        copy.wait()

    def place(slot):
        used = slot < live[0, 0]
        row = jnp.where(used, corners[slot, 0], 0)
        col = jnp.where(used, corners[slot, 1], 0)
        base = pl.multiple_of(col // 128 * 128, 128)
        return used, row, base, pl.multiple_of(base + WIDE, 128), col % 128

    def take(slot):
        _, row, base_re, base_im, shift = place(slot)
        back = (SPAN - shift) % SPAN
        columns = slice(SIDE * slot, SIDE * slot + SIDE)
        for i in range(4):
            here = slice(64 * i, 64 * i + 64)
            rows = pl.ds(pl.multiple_of(row + 64 * i, 8), 64)
            cell_re = pltpu.roll(cells[rows, pl.ds(base_re, SPAN)], back, 1)[:, :SIDE]
            cell_im = pltpu.roll(cells[rows, pl.ds(base_im, SPAN)], back, 1)[:, :SIDE]
            probe_re = probe[0, here, :]
            probe_im = probe[1, here, :]
            wave[here, columns] = (probe_re * cell_re - probe_im * cell_im).astype(jnp.bfloat16)
            wave[64 * i + SIDE:64 * i + SIDE + 64, columns] = (
                probe_re * cell_im + probe_im * cell_re).astype(jnp.bfloat16)

    def process(count):
        every = slice(0, SIDE * count)
        half_way = jnp.dot(left[...], wave[:, every], preferred_element_type=jnp.float32).astype(jnp.bfloat16)
        for e in range(count):
            columns = slice(SIDE * e, SIDE * e + SIDE)
            half[columns, :SIDE] = half_way[:SIDE, columns]
            half[columns, SIDE:] = half_way[SIDE:, columns]
        far = jnp.dot(half[every, :], right[...], preferred_element_type=jnp.float32)
        far_re = far[:, :SIDE]
        far_im = far[:, SIDE:]
        amplitude = pattern[0:count].reshape(count * SIDE, SIDE).astype(jnp.float32)
        ratio = amplitude * lax.rsqrt(far_re * far_re + far_im * far_im + 0.01)
        half[every, :SIDE] = (far_re * ratio).astype(jnp.bfloat16)
        half[every, SIDE:] = (far_im * ratio).astype(jnp.bfloat16)
        half_back = jnp.dot(half[every, :], left[...], preferred_element_type=jnp.float32).astype(jnp.bfloat16)
        for e in range(count):
            columns = slice(SIDE * e, SIDE * e + SIDE)
            wave[:SIDE, columns] = half_back[columns, :SIDE]
            wave[SIDE:, columns] = half_back[columns, SIDE:]
        near = jnp.dot(right[...], wave[:, every], preferred_element_type=jnp.float32)
        for e in range(count):
            used, row, base_re, base_im, shift = place(e)
            columns = slice(SIDE * e, SIDE * e + SIDE)
            for i in range(4):
                here = slice(64 * i, 64 * i + 64)
                rows = pl.ds(pl.multiple_of(row + 64 * i, 8), 64)
                near_re = near[64 * i:64 * i + 64, columns]
                near_im = near[64 * i + SIDE:64 * i + SIDE + 64, columns]
                probe_re = probe[0, here, :]
                probe_im = probe[1, here, :]
                blank = jnp.zeros((64, 128), jnp.float32)
                term_re = jnp.where(used, probe_re * near_re + probe_im * near_im, 0.0)
                term_im = jnp.where(used, probe_re * near_im - probe_im * near_re, 0.0)
                sums[rows, pl.ds(base_re, SPAN)] += pltpu.roll(jnp.concatenate([term_re, blank], 1), shift, 1)
                sums[rows, pl.ds(base_im, SPAN)] += pltpu.roll(jnp.concatenate([term_im, blank], 1), shift, 1)

    take(0)
    take(1)
    for copy in fetches[first_needs:]:
        copy.wait()

    @pl.when(live[0, 0] <= 2)
    def _():
        process(2)

    @pl.when(live[0, 0] > 2)
    def _():
        take(2)
        take(3)
        process(SLOTS)

    copies = []
    for y in range(WORKERS // 2):
        mine = pl.multiple_of(low_row(2 * y + core), LOW)
        other = pl.multiple_of(low_row(2 * y + 1 - core), LOW)
        own_mine = pl.multiple_of((2 * y + core) * OWN, OWN)
        own_other = pl.multiple_of((2 * y + 1 - core) * OWN, OWN)
        copies.append(pltpu.make_async_copy(sums.at[pl.ds(other, LOW)], send_low.at[y], sem.at[4 * y]))
        copies.append(pltpu.make_async_copy(sums.at[pl.ds(mine, LOW)], keep_low.at[y], sem.at[4 * y + 1]))
        copies.append(pltpu.make_async_copy(sums.at[pl.ds(own_other, OWN)], send_own.at[y], sem.at[4 * y + 2]))
        copies.append(pltpu.make_async_copy(sums.at[pl.ds(own_mine, OWN)], keep_own.at[y], sem.at[4 * y + 3]))
    for copy in copies:
        copy.start()
    for copy in copies:
        copy.wait()


def weight_kernel(corners, live, me, probe, weights, padded):
    padded[...] = jnp.zeros_like(padded)
    for i in range(4):
        here = slice(64 * i, 64 * i + 64)
        probe_re = probe[0, here, :]
        probe_im = probe[1, here, :]
        padded[PAD + 64 * i:PAD + 64 * i + 64, 0:SIDE] = probe_re * probe_re + probe_im * probe_im
    weights[...] = jnp.zeros_like(weights)
    own_first = me[0] * OWN

    def one(index, _):
        source = index // SLOTS
        slot = index % SLOTS
        used = slot < live[source]
        row = corners[source, 2 * slot] - jnp.where(source < WORKERS, 0, TILE)
        col = corners[source, 2 * slot + 1]
        first = own_first - row

        @pl.when(used & (first > -OWN) & (first < SIDE))
        def _():
            base = pl.multiple_of(col // 128 * 128, 128)
            piece = padded[pl.ds(pl.multiple_of(first + PAD, 8), OWN), :]
            weights[:, pl.ds(base, SPAN)] += pltpu.roll(piece, col % 128, 1)

        return 0

    lax.fori_loop(0, 2 * WORKERS * SLOTS, one, 0)


def low_kernel(parts, mirror_main, mirror_right, direct_main, direct_right):
    total = parts[0]
    for y in range(1, WORKERS // 2):
        total = total + parts[y]
    for main, right in ((mirror_main, mirror_right), (direct_main, direct_right)):
        main[:, :TILE] = total[:, :TILE]
        main[:, TILE:] = total[:, WIDE:WIDE + TILE]
        right[:, :SIDE] = total[:, TILE:WIDE]
        right[:, SIDE:] = total[:, WIDE + TILE:]


def smem():
    return pl.BlockSpec(memory_space=pltpu.SMEM)


def vmem():
    return pl.BlockSpec(memory_space=pltpu.VMEM)


def hbm():
    return pl.BlockSpec(memory_space=pl.ANY)


def patch_sums(corners, live, me, own_cells, low_mine, low_other, probe, patterns, left, right):
    own_chunk = jax.ShapeDtypeStruct((WORKERS // 2, OWN, 2 * WIDE), jnp.float32)
    low_chunk = jax.ShapeDtypeStruct((WORKERS // 2, LOW, 2 * WIDE), jnp.float32)
    return pl.pallas_call(
        slots_kernel,
        out_shape=(own_chunk, own_chunk, low_chunk, low_chunk),
        in_specs=[smem()] * 3 + [hbm()] * 7,
        out_specs=(hbm(), hbm(), hbm(), hbm()),
        scratch_shapes=[
            pltpu.VMEM((WIDE, 2 * WIDE), jnp.float32),
            pltpu.VMEM((WIDE, 2 * WIDE), jnp.float32),
            pltpu.VMEM((2 * SIDE, SLOTS * SIDE), jnp.bfloat16),
            pltpu.VMEM((SLOTS * SIDE, 2 * SIDE), jnp.bfloat16),
            pltpu.VMEM((2, SIDE, SIDE), jnp.float32),
            pltpu.VMEM((SLOTS, SIDE, SIDE), jnp.bfloat16),
            pltpu.VMEM((2 * SIDE, 2 * SIDE), jnp.bfloat16),
            pltpu.VMEM((2 * SIDE, 2 * SIDE), jnp.bfloat16),
            pltpu.SemaphoreType.DMA((5 + 2 * WORKERS,)),
        ],
        compiler_params=pltpu.CompilerParams(vmem_limit_bytes=51 * 2**20),
        cost_estimate=pl.CostEstimate(flops=2 * 10**9, bytes_accessed=12 * 10**6, transcendentals=0),
        name="patch_sums",
    )(corners, live, me, own_cells, low_mine, low_other, probe, patterns, left, right)


def weight_rows(corners, live, me, probe):
    return pl.pallas_call(
        weight_kernel,
        out_shape=jax.ShapeDtypeStruct((OWN, WIDE), jnp.float32),
        in_specs=[smem(), smem(), smem(), vmem()],
        out_specs=vmem(),
        scratch_shapes=[pltpu.VMEM((SIDE + 2 * PAD, SPAN), jnp.float32)],
        compiler_params=pltpu.CompilerParams(vmem_limit_bytes=16 * 2**20),
        cost_estimate=pl.CostEstimate(flops=10**7, bytes_accessed=10**6, transcendentals=0),
        name="weight_rows",
    )(corners, live, me, probe)


def low_sums(parts):
    return pl.pallas_call(
        low_kernel,
        out_shape=(
            jax.ShapeDtypeStruct((LOW, 2 * TILE), jnp.float32), jax.ShapeDtypeStruct((LOW, 2 * SIDE), jnp.float32)) * 2,
        in_specs=[vmem()],
        out_specs=(vmem(), vmem()) * 2,
        compiler_params=pltpu.CompilerParams(vmem_limit_bytes=8 * 2**20),
        cost_estimate=pl.CostEstimate(flops=2 * 10**5, bytes_accessed=10**6, transcendentals=0),
        name="low_sums",
    )(parts)


def moved(value, tile_step, pick):
    pairs = []
    for tile in range(TILES):
        for worker in range(WORKERS):
            target = pick(tile, worker)
            if target is not None and 0 <= tile + tile_step < TILES:
                pairs.append((tile * WORKERS + worker, (tile + tile_step) * WORKERS + target))
    return lax.ppermute(value, ("obj", "pat"), pairs)


def local(obj_tiles, probe_wave, amplitudes, offsets, live_count):
    own = obj_tiles[0]
    me = lax.axis_index("pat").astype(jnp.int32)
    corners = offsets[0, 0]

    mirrored = lambda worker: 2 * (7 - worker // 2) + worker % 2
    first_half = lambda tile, worker: worker if worker < 8 else None
    second_half = lambda tile, worker: mirrored(worker) if worker < 8 else None
    own_left = jnp.concatenate([own[0, :, :SIDE], own[1, :, :SIDE]], 1)
    from_right = moved(own_left, -1, lambda tile, worker: worker if tile % GRID_C else None)
    spare_re = jnp.zeros((OWN, 8), jnp.float32)
    spare_re = spare_re.at[0].set(corners.reshape(8).astype(jnp.float32))
    spare_re = spare_re.at[1].set(jnp.broadcast_to(live_count[0, 0].astype(jnp.float32), (8,)))
    shard = jnp.concatenate(
        [own[0], from_right[:, :SIDE - 8], spare_re, own[1], from_right[:, SIDE:]], 1)
    own_cells = lax.all_gather(shard, "pat", axis=0, tiled=True)
    low = moved(shard[:LOW], -GRID_C, first_half) + moved(shard[LOW:], -GRID_C, second_half)
    same_core = [list(range(0, WORKERS, 2)), list(range(1, WORKERS, 2))]
    sibling = [(i, i ^ 1) for i in range(WORKERS)]

    low_mine = lax.all_gather(low, "pat", axis=0, tiled=True, axis_index_groups=same_core)
    low_mine = low_mine.reshape(WORKERS // 2, LOW, 2 * WIDE)
    low_other = lax.ppermute(low_mine, "pat", sibling)

    left_table, right_table = dft_blocks(SIDE)
    keep_own, send_own, keep_low, send_low = patch_sums(
        corners, live_count, me.reshape(1), own_cells, low_mine, low_other, probe_wave, amplitudes[0, 0],
        left_table, right_table)
    other_low = lax.ppermute(send_low, "pat", sibling)
    other_own = lax.ppermute(send_own, "pat", sibling)
    both_own = (keep_own + other_own).reshape(WORKERS // 2 * OWN, 2 * WIDE)
    marks = own_cells.reshape(WORKERS, OWN, 2 * WIDE)[:, :2, WIDE - 8:WIDE].reshape(WORKERS, 16)
    both_own, other_low, marks = lax.optimization_barrier((both_own, other_low, marks))
    both_low = keep_low + other_low
    summed_own = lax.psum_scatter(
        both_own, "pat", scatter_dimension=0, tiled=True, axis_index_groups=same_core)

    upper_marks = moved(jnp.pad(marks, ((0, 0), (0, 112))), GRID_C, lambda tile, worker: worker)
    all_marks = jnp.concatenate([marks, upper_marks[:, :16]], 0).astype(jnp.int32)
    weights = weight_rows(all_marks[:, :8], all_marks[:, 8], me.reshape(1), probe_wave)

    mirror_main, mirror_right, direct_main, direct_right = low_sums(lax.all_to_all(both_low, "pat", 0, 0, axis_index_groups=same_core))

    def main_columns(rows, parts):
        return jnp.concatenate([rows[:, part * WIDE:part * WIDE + TILE] for part in range(parts)], 1)

    def right_columns(rows, parts):
        return jnp.concatenate([rows[:, part * WIDE + TILE:(part + 1) * WIDE] for part in range(parts)], 1)

    inside = lambda tile: tile % GRID_C != GRID_C - 1
    direct = lambda worker: worker if worker < 8 else None
    by_mirror = lambda worker: mirrored(worker) if worker >= 8 else None

    def pushed_down(main, right, pick):
        below = moved(main, GRID_C, lambda tile, worker: pick(worker))
        corner = moved(right, GRID_C + 1, lambda tile, worker: pick(worker) if inside(tile) else None)
        return below, corner

    def with_side(here, side):
        parts = []
        for part in range(here.shape[1] // TILE):
            first, cut, last = part * TILE, part * TILE + SIDE, (part + 1) * TILE
            parts += [here[:, first:cut] + side[:, part * SIDE:(part + 1) * SIDE], here[:, cut:last]]
        return jnp.concatenate(parts, 1)

    from_mirror = pushed_down(mirror_main, mirror_right, by_mirror)
    from_direct = pushed_down(direct_main, direct_right, direct)
    own_sums = jnp.concatenate([summed_own, weights], 1)
    from_left = moved(right_columns(own_sums, 3), 1, lambda tile, worker: worker if inside(tile) else None)
    main = main_columns(own_sums, 3)
    lower, top = lax.optimization_barrier((with_side(main[LOW:, :2 * TILE] + from_mirror[0], from_mirror[1]), main[:LOW, :2 * TILE]))
    top, lower = lax.optimization_barrier((top + from_direct[0], lower))
    lower, top = lax.optimization_barrier((
        with_side(lower, from_left[LOW:, :2 * SIDE]), with_side(top, from_left[:LOW, :2 * SIDE])))
    weight = with_side(main[:, 2 * TILE:], from_left[:, 2 * SIDE:])
    main = jnp.concatenate([with_side(top, from_direct[1]), lower], 0)

    over = 1.0 / (weight + 1.0)
    total = lambda part: main[:, part * TILE:(part + 1) * TILE]
    return jnp.stack([(total(part) - weight * own[part]) * over for part in range(2)])[None]


def solution(mesh):
    in_specs = (
        P("obj", None, "pat", None),
        P(),
        P("obj", "pat", None, None, None),
        P("obj", "pat", None, None),
        P("obj", "pat"),
    )
    out_specs = P("obj", None, "pat", None)
    return jax.shard_map(local, mesh=mesh, in_specs=in_specs, out_specs=out_specs, check_vma=False)
```
